32 devices in a mesh: dp: 4 (over y, core), seq: 8 (over z, x).
Axes of the slice: x: 2, y: 2, z: 4, core: 2. Of those that a mesh axis runs over, the one named last changes fastest.
Arguments:
- grad_out: bfloat16 [4, 1024, 4096], P('dp', 'seq'), may hold values from -6 to 6
- block_in: bfloat16 [4, 1024, 4096], P('dp', 'seq'), may hold values from -0.125 to 0.125
- residues: float32 [8, 4096], replicated, may hold values from -2 to 2
- decay_rates: float32 [8], replicated
Outputs:
- grad_in: bfloat16 [4, 1024, 4096], P('dp', 'seq')
- residue_grad: float32 [8, 4096], P(None, 'dp')
The draws below stay inside these ranges and needn't reach their ends.
All inputs are finite; a program needn't handle non-finite values.
Results may differ from the reference program's by a relative error of at most 0.0068.
Values sent between devices are 32-bit elements; how exact they have to be, the bound alone decides.
No kernel may reach another device: no remote copies, remote signals or barrier semaphores. Data moves between devices by JAX's collectives and lax.ppermute only.
A program may use at most 64 MiB of HBM per device.

```python
import math
import jax
import jax.numpy as jnp
from jax import lax

C = 4096
MODES = 8
LDEV = 128
BATCH = 4
L_TOTAL = 1024


def draw_decay_rates(key, part):
    pick_key, slow_key, fast_key = jax.random.split(key, 3)
    slow_share = 0.625
    total_length = L_TOTAL * 1.0
    fast_lowest = min(8.0 / total_length, 1.0 / 60.0)
    chosen = jax.random.uniform(pick_key, (MODES,)) < slow_share
    slow_rates = jnp.exp(jax.random.uniform(slow_key, (MODES,), minval=math.log(0.2 / total_length), maxval=math.log(6.0 / total_length)))
    fast_rates = jnp.exp(jax.random.uniform(fast_key, (MODES,), minval=math.log(fast_lowest), maxval=math.log(1.0 / 30.0)))
    return jnp.where(chosen, slow_rates, fast_rates).astype(jnp.float32)


def draw_grad_out(key, part):
    noise_key = jax.random.fold_in(jax.random.fold_in(key, 7), 0)
    period_key = jax.random.fold_in(jax.random.fold_in(key, 7), 2)
    phase_key = jax.random.fold_in(jax.random.fold_in(key, 7), 3)
    shape = (BATCH, L_TOTAL, C)
    noise = jax.random.truncated_normal(noise_key, -5.0, 5.0, shape)
    period = LDEV * jnp.exp(jax.random.uniform(period_key, (1, 1, C), minval=math.log(0.98), maxval=math.log(1.02)))
    phase = jax.random.uniform(phase_key, (BATCH, 1, C), minval=-math.pi, maxval=math.pi)
    positions = jnp.arange(L_TOTAL, dtype=jnp.float32)[None, :, None]
    wave = 0.5 * jnp.sin(2.0 * math.pi * positions / period + phase)
    return (noise + wave).astype(jnp.bfloat16)


def raised(result, rng, source, target, parts, factor):
    def block_of(dim):
        return (jnp.arange(result.shape[dim]) // (result.shape[dim] // parts)).reshape((-1,) + (1,) * (result.ndim - 1 - dim))

    first = jax.random.permutation(rng, parts)[block_of(target)]
    second = (block_of(target) + parts // 2) % parts
    return jnp.where((block_of(source) == first) | (block_of(source) == second), factor * result, result)


def level_of(rng, extent, cuts, low, largest):
    level, own = 1.0, jax.random.fold_in(rng, 6)
    for dim, shards_of in cuts:
        draws = jnp.exp(jax.random.uniform(jax.random.fold_in(own, dim), (shards_of,), jnp.float32, low / len(cuts), largest / len(cuts)))
        level = level * jnp.repeat(draws, extent[dim] // shards_of).reshape([-1 if axis == dim else 1 for axis in range(len(extent))])
    return level


def normal_values(key, dims, scale, reach, cuts=(), kind=jnp.bfloat16):
    result = scale * jax.random.normal(key, dims, jnp.float32)
    if cuts:
        result = result * level_of(key, dims, cuts, -0.22, 0.18)
    return jnp.clip(result, -reach, reach).astype(kind)


def bell_draw_with(stream_key, shape, deviation, most, cuts, heavy, held_as=jnp.bfloat16):
    values = deviation * jax.random.normal(stream_key, shape, jnp.float32)
    if cuts:
        values = values * level_of(stream_key, shape, cuts, -0.22, 0.18)
    return jnp.clip(raised(values, jax.random.fold_in(stream_key, 3), *heavy), -most, most).astype(held_as)


def setup_inputs(seed: int = 0) -> dict:
    seeds = jax.random.split(jax.random.key(seed), 5)
    return {
        "grad_out": draw_grad_out(jax.random.fold_in(seeds[4], 71), 0),
        "block_in": bell_draw_with(seeds[1], (BATCH, L_TOTAL, C), (BATCH * L_TOTAL) ** -0.5, 0.125, ((0, 4), (1, 8)), (0, 2, 4, 2.0)),
        "residues": normal_values(seeds[2], (MODES, C), MODES ** -0.5, 2.0, (), jnp.float32),
        "decay_rates": draw_decay_rates(jax.random.fold_in(seeds[4], 71), 0),
    }


def modal_tables(decay_rates, block_rows):
    offsets = jnp.arange(block_rows, dtype=jnp.float32)
    mode_gain = jnp.sqrt(1.0 - jnp.exp(-2.0 * decay_rates))
    lag_steps = offsets[None, :] - offsets[:, None]
    decay_table = jnp.where(lag_steps[None] >= 0, mode_gain[:, None, None] * jnp.exp(-decay_rates[:, None, None] * jnp.maximum(lag_steps[None], 0.0)), 0.0).astype(jnp.bfloat16)
    carry_table = (mode_gain[None, :] * jnp.exp(-decay_rates[None, :] * (block_rows - offsets[:, None]))).astype(jnp.bfloat16)
    state_table = jnp.exp(-decay_rates[:, None] * offsets[None, :]).astype(jnp.bfloat16)
    block_decay = jnp.exp(-decay_rates * block_rows)
    return (decay_table, carry_table, state_table, block_decay)

def local_terms(grad_out, block_in, residues, decay_table, carry_table, state_table):
    batch_rows, block_rows, channel_count = grad_out.shape
    mode_count = residues.shape[0]
    stacked_table = jnp.transpose(decay_table, (1, 0, 2)).reshape(block_rows, mode_count * block_rows)
    scaled = (grad_out[:, None, :, :] * residues[None, :, None, :]).astype(jnp.bfloat16).reshape(batch_rows, mode_count * block_rows, channel_count)
    local_grad = jnp.einsum('sk,bkc->bsc', stacked_table, scaled, preferred_element_type=jnp.float32)
    block_state = jnp.einsum('rt,btc->brc', state_table, grad_out, preferred_element_type=jnp.float32)
    pieces = []
    for mode_index in range(mode_count):
        weighted = jnp.einsum('st,bsc->btc', decay_table[mode_index], block_in, preferred_element_type=jnp.float32)
        pieces.append(lax.optimization_barrier(jnp.sum(weighted * grad_out, axis=(0, 1))))
    local_part = jnp.stack(pieces)
    carry_weights = jnp.einsum('sr,bsc->brc', carry_table, block_in, preferred_element_type=jnp.float32)
    return (local_grad, block_state, local_part, carry_weights)

def reference(grad_out, block_in, residues, decay_rates):
    batch_rows, length, channel_count = grad_out.shape
    block_rows = LDEV
    block_count = length // block_rows
    mode_count = residues.shape[0]
    decay_table, carry_table, state_table, block_decay = modal_tables(decay_rates, block_rows)

    def blocks(array):
        return array.reshape(batch_rows, block_count, block_rows, channel_count).transpose(1, 0, 2, 3)

    def advance(incoming, pair):
        dy_block, in_block = pair
        local_grad, block_state, local_part, carry_weights = local_terms(dy_block, in_block, residues, decay_table, carry_table, state_table)
        carried = jnp.einsum('sr,brc->bsc', carry_table.astype(jnp.float32), residues[None] * incoming, precision=lax.Precision.HIGHEST)
        grad_block = (local_grad + carried).astype(jnp.bfloat16)
        part_sum = local_part + lax.optimization_barrier(jnp.sum(incoming * carry_weights, axis=0))
        following = block_state + block_decay[None, :, None] * incoming
        return (following, (grad_block, part_sum))
    start_state = jnp.zeros((batch_rows, mode_count, channel_count), jnp.float32)
    final_state, outputs = lax.scan(advance, start_state, (blocks(grad_out), blocks(block_in)), reverse=True)
    grad_blocks, part_sums = outputs
    grad_in = grad_blocks.transpose(1, 0, 2, 3).reshape(batch_rows, length, channel_count)
    return (grad_in, lax.optimization_barrier(jnp.sum(part_sums, axis=0)))
```

```python
import functools

import jax
import jax.numpy as jnp
from jax import lax
from jax.experimental import pallas as pl
from jax.experimental.pallas import tpu as pltpu
from jax.sharding import PartitionSpec as P

VMEM_LIMIT = 48 * 1024 * 1024
LANES = 128


def rate_column(rates_ref, mode_count, width):
    rows = lax.broadcasted_iota(jnp.int32, (mode_count, width), 0)
    column = jnp.zeros((mode_count, width), jnp.float32)
    for r in range(mode_count):
        column = jnp.where(rows == r, rates_ref[r], column)
    return column


def mode_gain(rates):
    return jnp.sqrt(1.0 - jnp.exp(-2.0 * rates))


def decay_matrix(rate, rows, earlier_first):
    down = lax.broadcasted_iota(jnp.int32, (rows, rows), 0)
    across = lax.broadcasted_iota(jnp.int32, (rows, rows), 1)
    lag = (across - down if earlier_first else down - across).astype(jnp.float32)
    rates = jnp.full((rows, rows), rate, jnp.float32)
    gain = mode_gain(jnp.full((8, rows), rate, jnp.float32))[:1]
    table = gain * jnp.exp(-rates * jnp.maximum(lag, 0.0))
    return jnp.where(lag >= 0.0, table, 0.0).astype(jnp.bfloat16)


def terms_kernel(sub, rates_ref, grad_ref, in_ref, out_ref, decay_ref, pair_ref):
    mode_count = rates_ref.shape[0]
    rows, width = grad_ref.shape[1:]

    @pl.when(pl.program_id(0) == 0)
    def _():
        for r in range(mode_count):
            decay_ref[r * rows : (r + 1) * rows, :] = decay_matrix(rates_ref[r], rows, False)
        rates = rate_column(rates_ref, mode_count, rows)
        offset = lax.broadcasted_iota(jnp.int32, (mode_count, rows), 1).astype(jnp.float32)
        state = jnp.exp(-rates * offset)
        carry = mode_gain(rates) * jnp.exp(-rates * (rows - offset))
        pair_ref[...] = jnp.concatenate([state, carry], axis=0).astype(jnp.bfloat16)

    for first in range(0, width, sub):
        part = slice(first, first + sub)
        grad = grad_ref[0, :, part]
        block = in_ref[0, :, part]
        state = jnp.dot(pair_ref[...], grad, preferred_element_type=jnp.float32)[:mode_count]
        carry = jnp.dot(pair_ref[...], block, preferred_element_type=jnp.float32)[mode_count:]
        grad32 = grad.astype(jnp.float32)
        sums = []
        for r in range(mode_count):
            weighted = jnp.dot(
                decay_ref[r * rows : (r + 1) * rows, :], block, preferred_element_type=jnp.float32
            )
            sums.append(jnp.sum(weighted * grad32, axis=0, keepdims=True))
        local = jnp.concatenate(sums, axis=0)
        for k in range(sub // LANES):
            lanes = slice(k * LANES, (k + 1) * LANES)
            chunk = first // LANES + k
            out_ref[chunk, 0:mode_count, :] = state[:, lanes]
            out_ref[chunk, mode_count : 2 * mode_count, :] = carry[:, lanes]
            out_ref[chunk, 2 * mode_count : 3 * mode_count, :] = local[:, lanes]


def local_grad_kernel(sub, rates_ref, residues_ref, grad_ref, out_ref, decay_ref):
    mode_count = rates_ref.shape[0]
    rows, width = grad_ref.shape[1:]

    @pl.when(pl.program_id(0) == 0)
    def _():
        for r in range(mode_count):
            decay_ref[:, r * rows : (r + 1) * rows] = decay_matrix(rates_ref[r], rows, True)

    for first in range(0, width, sub):
        part = slice(first, first + sub)
        grad32 = grad_ref[0, :, part].astype(jnp.float32)
        scaled = jnp.concatenate(
            [
                (grad32 * residues_ref[r : r + 1, part]).astype(jnp.bfloat16)
                for r in range(mode_count)
            ],
            axis=0,
        )
        out_ref[:, part] = jnp.dot(decay_ref[...], scaled, preferred_element_type=jnp.float32)


def scan_kernel(batch_count, block_count, rates_ref, terms_ref, out_ref):
    mode_count = rates_ref.shape[0]
    width = terms_ref.shape[2]
    block_rows = LANES
    decay = jnp.exp(-rate_column(rates_ref, mode_count, width) * block_rows)
    zero = jnp.zeros((mode_count, width), jnp.float32)

    def sequence(b, total):
        def block(j, state):
            total, incoming = state
            at = (b + 1) * block_count - 1 - j
            out_ref[at, 0:mode_count, :] = incoming
            carry = terms_ref[at, mode_count : 2 * mode_count, :]
            total = total + (terms_ref[at, 2 * mode_count : 3 * mode_count, :] + incoming * carry)
            return total, terms_ref[at, 0:mode_count, :] + decay * incoming

        return lax.fori_loop(0, block_count, block, (total, zero), unroll=block_count <= 8)[0]

    total = lax.fori_loop(0, batch_count, sequence, zero, unroll=batch_count <= 8)

    def spread(at, carry):
        out_ref[at, mode_count : 2 * mode_count, :] = total
        return carry

    lax.fori_loop(0, batch_count * block_count, spread, 0, unroll=8)


def finish_kernel(rates_ref, residues_ref, local_ref, back_ref, grad_ref, sum_ref):
    mode_count = rates_ref.shape[0]
    rows, width = local_ref.shape
    step = pl.program_id(0)
    chunks = width // LANES
    rates = rate_column(rates_ref, mode_count, rows)
    offset = lax.broadcasted_iota(jnp.int32, (mode_count, rows), 1).astype(jnp.float32)
    carry = mode_gain(rates) * jnp.exp(-rates * (rows - offset))
    carry3 = jnp.concatenate([carry, carry, carry], axis=0).astype(jnp.bfloat16)
    pieces = []
    for k in range(chunks):
        lanes = slice(k * LANES, (k + 1) * LANES)
        rest = residues_ref[:, lanes] * back_ref[step * chunks + k, 0:mode_count, :]
        split = []
        for _ in range(3):
            split.append(rest.astype(jnp.bfloat16).astype(jnp.float32))
            rest = rest - split[-1]
        pieces.append(jnp.concatenate(split, axis=0).astype(jnp.bfloat16))
    carried = lax.dot_general(
        carry3,
        jnp.concatenate(pieces, axis=1),
        (((0,), (0,)), ((), ())),
        preferred_element_type=jnp.float32,
    )
    grad_ref[0] = (local_ref[...] + carried).astype(jnp.bfloat16)

    @pl.when(step == 0)
    def _():
        own = sum_ref.shape[1] // LANES
        base = lax.axis_index("dp") * own
        for k in range(own):
            sum_ref[:, k * LANES : (k + 1) * LANES] = back_ref[base + k, mode_count : 2 * mode_count, :]


def to_owners(chunks, owners):
    count, rows, lanes = chunks.shape
    if owners == count:
        return chunks
    narrow = count * lanes // owners
    parts = chunks.reshape(count, rows, lanes // narrow, narrow)
    return jnp.swapaxes(parts, 1, 2).reshape(owners, rows, narrow)


def from_owners(parts, count):
    owners, rows, narrow = parts.shape
    if owners == count:
        return parts
    chunks = parts.reshape(count, owners // count, rows, narrow)
    return jnp.swapaxes(chunks, 1, 2).reshape(count, rows, LANES)


def params():
    return pltpu.CompilerParams(vmem_limit_bytes=VMEM_LIMIT)


def local(batch_count, block_count, grad_out, block_in, residues, decay_rates):
    _, rows, channels = grad_out.shape
    modes = residues.shape[0]
    owners = batch_count * block_count
    smem = pl.BlockSpec(memory_space=pltpu.SMEM)
    width = 1024
    steps = channels // width
    rows_block = pl.BlockSpec((1, rows, width), lambda i: (0, 0, i))
    terms = pl.pallas_call(
        functools.partial(terms_kernel, 256),
        grid=(steps,),
        in_specs=[smem, rows_block, rows_block],
        out_specs=pl.BlockSpec((width // LANES, 3 * modes, LANES), lambda i: (i, 0, 0)),
        out_shape=jax.ShapeDtypeStruct((channels // LANES, 3 * modes, LANES), jnp.float32),
        scratch_shapes=[
            pltpu.VMEM((modes * rows, rows), jnp.bfloat16),
            pltpu.VMEM((2 * modes, rows), jnp.bfloat16),
        ],
        compiler_params=params(),
        name="terms",
    )(decay_rates, grad_out, block_in)
    terms = lax.all_to_all(to_owners(terms, owners), ("dp", "seq"), 0, 0)
    local_grad = pl.pallas_call(
        functools.partial(local_grad_kernel, 256),
        grid=(steps,),
        in_specs=[smem, pl.BlockSpec((modes, width), lambda i: (0, i)), rows_block],
        out_specs=pl.BlockSpec((rows, width), lambda i: (0, i)),
        out_shape=jax.ShapeDtypeStruct((rows, channels), jnp.float32),
        scratch_shapes=[pltpu.VMEM((rows, modes * rows), jnp.bfloat16)],
        compiler_params=params(),
        cost_estimate=pl.CostEstimate(
            flops=2 * rows * modes * rows * channels,
            bytes_accessed=6 * rows * channels,
            transcendentals=0,
        ),
        name="local_grad",
    )(decay_rates, residues, grad_out)
    whole = pl.BlockSpec(memory_space=pltpu.VMEM)
    back = pl.pallas_call(
        functools.partial(scan_kernel, batch_count, block_count),
        in_specs=[smem, whole],
        out_specs=whole,
        out_shape=jax.ShapeDtypeStruct((owners, 2 * modes, channels // owners), jnp.float32),
        compiler_params=params(),
        name="scan",
    )(decay_rates, terms)
    back = from_owners(lax.all_to_all(back, ("dp", "seq"), 0, 0), channels // LANES)
    return pl.pallas_call(
        finish_kernel,
        grid=(steps,),
        in_specs=[
            smem,
            pl.BlockSpec((modes, width), lambda i: (0, i)),
            pl.BlockSpec((rows, width), lambda i: (0, i)),
            pl.BlockSpec((channels // LANES, 2 * modes, LANES), lambda i: (0, 0, 0)),
        ],
        out_specs=[rows_block, pl.BlockSpec((modes, channels // batch_count), lambda i: (0, 0))],
        out_shape=[
            jax.ShapeDtypeStruct((1, rows, channels), jnp.bfloat16),
            jax.ShapeDtypeStruct((modes, channels // batch_count), jnp.float32),
        ],
        compiler_params=params(),
        name="finish",
    )(decay_rates, residues, local_grad, back)


def solution(mesh):
    placed = (P("dp", "seq", None), P("dp", "seq", None), P(), P())
    return jax.shard_map(
        functools.partial(local, mesh.shape["dp"], mesh.shape["seq"]),
        mesh=mesh,
        in_specs=placed,
        out_specs=(P("dp", "seq", None), P(None, "dp")),
        check_vma=False,
    )
```

```python
import functools

import jax
import jax.numpy as jnp
from jax import lax
from jax.experimental import pallas as pl
from jax.experimental.pallas import tpu as pltpu
from jax.sharding import PartitionSpec as P

VMEM_LIMIT = 48 * 1024 * 1024
FIRST_LIMIT = 60 * 1024 * 1024
LANES = 128


def rate_column(rates_ref, mode_count, width):
    rows = lax.broadcasted_iota(jnp.int32, (mode_count, width), 0)
    column = jnp.zeros((mode_count, width), jnp.float32)
    for r in range(mode_count):
        column = jnp.where(rows == r, rates_ref[r], column)
    return column


def mode_gain(rates):
    return jnp.sqrt(1.0 - jnp.exp(-2.0 * rates))


def decay_matrix(rate, rows, earlier_first):
    down = lax.broadcasted_iota(jnp.int32, (rows, rows), 0)
    across = lax.broadcasted_iota(jnp.int32, (rows, rows), 1)
    lag = (across - down if earlier_first else down - across).astype(jnp.float32)
    rates = jnp.full((rows, rows), rate, jnp.float32)
    gain = mode_gain(jnp.full((8, rows), rate, jnp.float32))[:1]
    table = gain * jnp.exp(-rates * jnp.maximum(lag, 0.0))
    return jnp.where(lag >= 0.0, table, 0.0).astype(jnp.bfloat16)


def terms_kernel(
    slices, sub, rates_hbm, grad_hbm, in_hbm, out_ref, rates_ref, grad_ref, in_ref, decay_ref, pair_ref, sems
):
    mode_count = rates_ref.shape[0]
    rows, channels = grad_ref.shape
    width = channels // slices
    get_rates = pltpu.make_async_copy(rates_hbm, rates_ref, sems.at[2, 0])
    get_rates.start()
    loads = []
    for i in range(slices):
        part = pl.ds(i * width, width)
        pair = (
            pltpu.make_async_copy(grad_hbm.at[0, :, part], grad_ref.at[:, part], sems.at[0, i]),
            pltpu.make_async_copy(in_hbm.at[0, :, part], in_ref.at[:, part], sems.at[1, i]),
        )
        for copy in pair:
            copy.start()
        loads.append(pair)
    get_rates.wait()
    for r in range(mode_count):
        decay_ref[r * rows : (r + 1) * rows, :] = decay_matrix(rates_ref[r], rows, False)
    rates = rate_column(rates_ref, mode_count, rows)
    offset = lax.broadcasted_iota(jnp.int32, (mode_count, rows), 1).astype(jnp.float32)
    state = jnp.exp(-rates * offset)
    carry = mode_gain(rates) * jnp.exp(-rates * (rows - offset))
    pair_ref[...] = jnp.concatenate([state, carry], axis=0).astype(jnp.bfloat16)

    for i in range(slices):
        for copy in loads[i]:
            copy.wait()
        for first in range(i * width, (i + 1) * width, sub):
            part = slice(first, first + sub)
            grad = grad_ref[:, part]
            block = in_ref[:, part]
            state = jnp.dot(pair_ref[...], grad, preferred_element_type=jnp.float32)[:mode_count]
            carry = jnp.dot(pair_ref[...], block, preferred_element_type=jnp.float32)[mode_count:]
            grad32 = grad.astype(jnp.float32)
            weighted = jnp.dot(decay_ref[...], block, preferred_element_type=jnp.float32)
            local = jnp.concatenate(
                [
                    jnp.sum(weighted[r * rows : (r + 1) * rows] * grad32, axis=0, keepdims=True)
                    for r in range(mode_count)
                ],
                axis=0,
            )
            for k in range(sub // LANES):
                lanes = slice(k * LANES, (k + 1) * LANES)
                chunk = first // LANES + k
                out_ref[chunk, 0:mode_count, :] = state[:, lanes]
                out_ref[chunk, mode_count : 2 * mode_count, :] = carry[:, lanes]
                out_ref[chunk, 2 * mode_count : 3 * mode_count, :] = local[:, lanes]


def local_grad_kernel(sub, rates_ref, residues_ref, grad_ref, out_ref, decay_ref):
    mode_count = rates_ref.shape[0]
    rows, width = grad_ref.shape[1:]

    @pl.when(pl.program_id(0) == 0)
    def _():
        for r in range(mode_count):
            decay_ref[:, r * rows : (r + 1) * rows] = decay_matrix(rates_ref[r], rows, True)

    for first in range(0, width, sub):
        part = slice(first, first + sub)
        grad32 = grad_ref[0, :, part].astype(jnp.float32)
        scaled = jnp.concatenate(
            [
                (grad32 * residues_ref[r : r + 1, part]).astype(jnp.bfloat16)
                for r in range(mode_count)
            ],
            axis=0,
        )
        out_ref[:, part] = jnp.dot(decay_ref[...], scaled, preferred_element_type=jnp.float32)


def scan_kernel(batch_count, block_count, rates_ref, terms_ref, out_ref):
    mode_count = rates_ref.shape[0]
    width = terms_ref.shape[2]
    block_rows = LANES
    decay = jnp.exp(-rate_column(rates_ref, mode_count, width) * block_rows)
    zero = jnp.zeros((mode_count, width), jnp.float32)

    def sequence(b, total):
        def block(j, state):
            total, incoming = state
            at = (b + 1) * block_count - 1 - j
            out_ref[at, 0:mode_count, :] = incoming
            carry = terms_ref[at, mode_count : 2 * mode_count, :]
            total = total + (terms_ref[at, 2 * mode_count : 3 * mode_count, :] + incoming * carry)
            return total, terms_ref[at, 0:mode_count, :] + decay * incoming

        return lax.fori_loop(0, block_count, block, (total, zero), unroll=block_count <= 8)[0]

    total = lax.fori_loop(0, batch_count, sequence, zero, unroll=batch_count <= 8)

    def spread(at, carry):
        out_ref[at, mode_count : 2 * mode_count, :] = total
        return carry

    lax.fori_loop(0, batch_count * block_count, spread, 0, unroll=8)


def finish_kernel(
    slices, rates_ref, residues_ref, local_ref, back_ref, grad_hbm, sum_ref, grad_ref, sems
):
    mode_count = rates_ref.shape[0]
    rows, channels = local_ref.shape
    width = channels // slices
    rates = rate_column(rates_ref, mode_count, rows)
    offset = lax.broadcasted_iota(jnp.int32, (mode_count, rows), 1).astype(jnp.float32)
    carry = mode_gain(rates) * jnp.exp(-rates * (rows - offset))
    carry_twice = jnp.concatenate([carry, carry], axis=0).astype(jnp.bfloat16)
    stores = []
    for i in range(slices):
        pieces = []
        for chunk in range(i * width // LANES, (i + 1) * width // LANES):
            lanes = slice(chunk * LANES, (chunk + 1) * LANES)
            value = residues_ref[:, lanes] * back_ref[chunk, 0:mode_count, :]
            high = value.astype(jnp.bfloat16).astype(jnp.float32)
            pieces.append(jnp.concatenate([high, value - high], axis=0).astype(jnp.bfloat16))
        carried = lax.dot_general(
            carry_twice,
            jnp.concatenate(pieces, axis=1),
            (((0,), (0,)), ((), ())),
            preferred_element_type=jnp.float32,
        )
        part = pl.ds(i * width, width)
        grad_ref[:, part] = (local_ref[:, part] + carried).astype(jnp.bfloat16)
        stores.append(
            pltpu.make_async_copy(grad_ref.at[:, part], grad_hbm.at[0, :, part], sems.at[i])
        )
        stores[-1].start()
    own = sum_ref.shape[1] // LANES
    base = lax.axis_index("dp") * own
    for k in range(own):
        sum_ref[:, k * LANES : (k + 1) * LANES] = back_ref[base + k, mode_count : 2 * mode_count, :]
    for copy in stores:
        copy.wait()


def to_owners(chunks, owners):
    count, rows, lanes = chunks.shape
    if owners == count:
        return chunks
    narrow = count * lanes // owners
    parts = chunks.reshape(count, rows, lanes // narrow, narrow)
    return jnp.swapaxes(parts, 1, 2).reshape(owners, rows, narrow)


def from_owners(parts, count):
    owners, rows, narrow = parts.shape
    if owners == count:
        return parts
    chunks = parts.reshape(count, owners // count, rows, narrow)
    return jnp.swapaxes(chunks, 1, 2).reshape(count, rows, LANES)


def params(limit=VMEM_LIMIT):
    return pltpu.CompilerParams(vmem_limit_bytes=limit)


def local(batch_count, block_count, grad_out, block_in, residues, decay_rates):
    _, rows, channels = grad_out.shape
    modes = residues.shape[0]
    owners = batch_count * block_count
    smem = pl.BlockSpec(memory_space=pltpu.SMEM)
    width = 1024
    steps = channels // width
    rows_block = pl.BlockSpec((1, rows, width), lambda i: (0, 0, i))
    anywhere = pl.BlockSpec(memory_space=pl.ANY)
    whole = pl.BlockSpec(memory_space=pltpu.VMEM)
    terms = pl.pallas_call(
        functools.partial(terms_kernel, steps, 256),
        in_specs=[anywhere, anywhere, anywhere],
        out_specs=whole,
        out_shape=jax.ShapeDtypeStruct((channels // LANES, 3 * modes, LANES), jnp.float32),
        scratch_shapes=[
            pltpu.SMEM((modes,), jnp.float32),
            pltpu.VMEM((rows, channels), jnp.bfloat16),
            pltpu.VMEM((rows, channels), jnp.bfloat16),
            pltpu.VMEM((modes * rows, rows), jnp.bfloat16),
            pltpu.VMEM((2 * modes, rows), jnp.bfloat16),
            pltpu.SemaphoreType.DMA((3, steps)),
        ],
        compiler_params=params(FIRST_LIMIT),
        name="terms",
    )(decay_rates, grad_out, block_in)
    terms = lax.all_to_all(to_owners(terms, owners), ("dp", "seq"), 0, 0)
    local_grad = pl.pallas_call(
        functools.partial(local_grad_kernel, 256),
        grid=(steps,),
        in_specs=[smem, pl.BlockSpec((modes, width), lambda i: (0, i)), rows_block],
        out_specs=pl.BlockSpec((rows, width), lambda i: (0, i)),
        out_shape=jax.ShapeDtypeStruct((rows, channels), jnp.float32),
        scratch_shapes=[pltpu.VMEM((rows, modes * rows), jnp.bfloat16)],
        compiler_params=params(),
        cost_estimate=pl.CostEstimate(
            flops=2 * rows * modes * rows * channels,
            bytes_accessed=6 * rows * channels,
            transcendentals=0,
        ),
        name="local_grad",
    )(decay_rates, residues, grad_out)
    back = pl.pallas_call(
        functools.partial(scan_kernel, batch_count, block_count),
        in_specs=[smem, whole],
        out_specs=whole,
        out_shape=jax.ShapeDtypeStruct((owners, 2 * modes, channels // owners), jnp.float32),
        compiler_params=params(),
        name="scan",
    )(decay_rates, terms)
    back = from_owners(lax.all_to_all(back, ("dp", "seq"), 0, 0), channels // LANES)
    return pl.pallas_call(
        functools.partial(finish_kernel, steps),
        in_specs=[smem, whole, whole, whole],
        out_specs=[anywhere, whole],
        out_shape=[
            jax.ShapeDtypeStruct((1, rows, channels), jnp.bfloat16),
            jax.ShapeDtypeStruct((modes, channels // batch_count), jnp.float32),
        ],
        scratch_shapes=[pltpu.VMEM((rows, channels), jnp.bfloat16), pltpu.SemaphoreType.DMA((steps,))],
        compiler_params=params(),
        name="finish",
    )(decay_rates, residues, local_grad, back)


def solution(mesh):
    placed = (P("dp", "seq", None), P("dp", "seq", None), P(), P())
    return jax.shard_map(
        functools.partial(local, mesh.shape["dp"], mesh.shape["seq"]),
        mesh=mesh,
        in_specs=placed,
        out_specs=(P("dp", "seq", None), P(None, "dp")),
        check_vma=False,
    )
```

```python
import functools

import jax
import jax.numpy as jnp
from jax import lax
from jax.experimental import pallas as pl
from jax.experimental.pallas import tpu as pltpu
from jax.sharding import PartitionSpec as P

VMEM_LIMIT = 48 * 1024 * 1024
FIRST_LIMIT = 60 * 1024 * 1024
LANES = 128
SUBLANES = 8
GROUP = 4


def rate_column(rates_ref, mode_count, width):
    rows = lax.broadcasted_iota(jnp.int32, (mode_count, width), 0)
    column = jnp.zeros((mode_count, width), jnp.float32)
    for r in range(mode_count):
        column = jnp.where(rows == r, rates_ref[r], column)
    return column


def mode_gain(rates):
    return jnp.sqrt(1.0 - jnp.exp(-2.0 * rates))


def decay_matrix(rate, rows):
    earlier = lax.broadcasted_iota(jnp.int32, (rows, rows), 0)
    later = lax.broadcasted_iota(jnp.int32, (rows, rows), 1)
    lag = (later - earlier).astype(jnp.float32)
    rates = jnp.full((rows, rows), rate, jnp.float32)
    gain = mode_gain(jnp.full((SUBLANES, rows), rate, jnp.float32))[:1]
    table = gain * jnp.exp(-rates * jnp.maximum(lag, 0.0))
    return jnp.where(lag >= 0.0, table, 0.0).astype(jnp.bfloat16)


def split_bf16(value):
    high = value.astype(jnp.bfloat16)
    return high, (value - high.astype(jnp.float32)).astype(jnp.bfloat16)


def terms_kernel(
    slices,
    sub,
    rates_hbm,
    grad_hbm,
    in_hbm,
    out_ref,
    rates_ref,
    grad_ref,
    in_ref,
    before_ref,
    after_ref,
    lag_ref,
    sems,
):
    modes = rates_ref.shape[0]
    rows, channels = grad_ref.shape
    width = channels // slices
    groups = rows // GROUP
    get_rates = pltpu.make_async_copy(rates_hbm, rates_ref, sems.at[2, 0])
    get_rates.start()
    loads = []
    for i in range(slices):
        part = pl.ds(i * width, width)
        pair = (
            pltpu.make_async_copy(grad_hbm.at[0, :, part], grad_ref.at[:, part], sems.at[0, i]),
            pltpu.make_async_copy(in_hbm.at[0, :, part], in_ref.at[:, part], sems.at[1, i]),
        )
        for copy in pair:
            copy.start()
        loads.append(pair)
    get_rates.wait()
    rates = rate_column(rates_ref, modes, rows)
    gain = mode_gain(rates)
    position = lax.broadcasted_iota(jnp.int32, (modes, rows), 1)
    offset = position.astype(jnp.float32)
    for u in range(1, groups + 1):
        at = slice((u - 1) * modes, u * modes)
        edge = u * GROUP
        before = gain * jnp.exp(-rates * jnp.maximum(edge - offset, 0.0))
        if u < groups:
            after = jnp.exp(-rates * jnp.maximum(offset - edge, 0.0))
            after = jnp.where((position >= edge) & (position < edge + GROUP), after, 0.0)
            high, low = split_bf16(jnp.where(position < edge, before, 0.0))
            after_high, after_low = split_bf16(after)
        else:
            high, low = before.astype(jnp.bfloat16), jnp.zeros((modes, rows), jnp.bfloat16)
            after_high, after_low = jnp.exp(-rates * offset).astype(jnp.bfloat16), low
        before_ref[at, 0:rows] = high
        before_ref[at, rows : 2 * rows] = low
        after_ref[at, 0:rows] = after_high
        after_ref[at, rows : 2 * rows] = after_low
    for k in range(GROUP):
        lag_ref[k] = (gain * jnp.exp(-rates * k))[:, :LANES]

    in_group = lax.broadcasted_iota(jnp.int32, (SUBLANES, sub), 0) % GROUP
    for i in range(slices):
        for copy in loads[i]:
            copy.wait()
        for first in range(i * width, (i + 1) * width, sub):
            part = slice(first, first + sub)
            grad = grad_ref[:, part]
            block = in_ref[:, part]
            twice = jnp.concatenate([block, block], axis=0)
            sums = jnp.dot(before_ref[...], twice, preferred_element_type=jnp.float32)
            twice = jnp.concatenate([grad, grad], axis=0)
            states = jnp.dot(after_ref[...], twice, preferred_element_type=jnp.float32)
            last = slice((groups - 1) * modes, groups * modes)
            carry, state = sums[last], states[last]
            local = sums[0:modes] * states[0:modes]
            for u in range(1, groups - 1):
                at = slice(u * modes, (u + 1) * modes)
                local = local + sums[at] * states[at]
            grad32 = grad.astype(jnp.float32).reshape(rows // SUBLANES, SUBLANES, sub)
            block32 = block.astype(jnp.float32).reshape(rows // SUBLANES, SUBLANES, sub)
            for k in range(GROUP):
                later = pltpu.roll(grad32, SUBLANES - k, 1) if k else grad32
                product = jnp.sum(block32 * later, axis=0)
                if k:
                    product = jnp.where(in_group + k < GROUP, product, 0.0)
                weight = jnp.concatenate([lag_ref[k]] * (sub // LANES), axis=1)
                local = local + weight * jnp.sum(product, axis=0, keepdims=True)
            for k in range(sub // LANES):
                lanes = slice(k * LANES, (k + 1) * LANES)
                chunk = first // LANES + k
                out_ref[chunk, 0:modes, :] = state[:, lanes]
                out_ref[chunk, modes : 2 * modes, :] = carry[:, lanes]
                out_ref[chunk, 2 * modes : 3 * modes, :] = local[:, lanes]


def local_grad_kernel(
    sub, rates_hbm, residues_ref, grad_hbm, out_ref, rates_ref, grad_ref, decay_ref, sems
):
    modes = rates_ref.shape[0]
    rows, channels = grad_ref.shape
    get_rates = pltpu.make_async_copy(rates_hbm, rates_ref, sems.at[0])
    get_rates.start()
    get_grad = pltpu.make_async_copy(grad_hbm.at[0], grad_ref, sems.at[1])
    get_grad.start()
    get_rates.wait()
    for r in range(modes):
        decay_ref[:, r * rows : (r + 1) * rows] = decay_matrix(rates_ref[r], rows)
    column = lax.broadcasted_iota(jnp.int32, (rows, LANES), 1) % modes
    rates = jnp.zeros((rows, LANES), jnp.float32)
    for r in range(modes):
        rates = jnp.where(column == r, rates_ref[r], rates)
    offset = lax.broadcasted_iota(jnp.int32, (rows, LANES), 0).astype(jnp.float32)
    out_ref[:, channels : channels + LANES] = mode_gain(rates) * jnp.exp(-rates * (rows - offset))
    rates = rate_column(rates_ref, modes, LANES)
    out_ref[0:modes, channels + LANES : channels + 2 * LANES] = jnp.exp(-rates * rows)
    get_grad.wait()

    @pl.loop(0, channels // sub)
    def _(i):
        part = pl.ds(pl.multiple_of(i * sub, sub), sub)
        grad32 = grad_ref[:, part].astype(jnp.float32)
        scaled = jnp.concatenate(
            [(grad32 * residues_ref[r : r + 1, part]).astype(jnp.bfloat16) for r in range(modes)],
            axis=0,
        )
        out_ref[:, part] = jnp.dot(decay_ref[...], scaled, preferred_element_type=jnp.float32)


def scan_kernel(batch_count, block_count, local_ref, terms_ref, out_ref):
    mode_count = out_ref.shape[1] // 2
    width = terms_ref.shape[2]
    last = local_ref.shape[1] - LANES
    decay = local_ref[0:mode_count, last : last + width]
    zero = jnp.zeros((mode_count, width), jnp.float32)

    def sequence(b, total):
        def block(j, state):
            total, incoming = state
            at = (b + 1) * block_count - 1 - j
            out_ref[at, 0:mode_count, :] = incoming
            carry = terms_ref[at, mode_count : 2 * mode_count, :]
            total = total + (terms_ref[at, 2 * mode_count : 3 * mode_count, :] + incoming * carry)
            return total, terms_ref[at, 0:mode_count, :] + decay * incoming

        return lax.fori_loop(0, block_count, block, (total, zero), unroll=block_count <= 8)[0]

    total = lax.fori_loop(0, batch_count, sequence, zero, unroll=batch_count <= 8)

    def spread(at, carry):
        out_ref[at, mode_count : 2 * mode_count, :] = total
        return carry

    lax.fori_loop(0, batch_count * block_count, spread, 0, unroll=8)


def finish_kernel(slices, residues_ref, local_ref, back_ref, grad_hbm, sum_ref, grad_ref, sems):
    modes, channels = residues_ref.shape
    rows = local_ref.shape[0]
    width = channels // slices
    carry = local_ref[:, channels : channels + 2 * modes].astype(jnp.bfloat16)
    stores = []
    for i in range(slices):
        pieces = []
        for chunk in range(i * width // LANES, (i + 1) * width // LANES):
            lanes = slice(chunk * LANES, (chunk + 1) * LANES)
            value = residues_ref[:, lanes] * back_ref[chunk, 0:modes, :]
            high = value.astype(jnp.bfloat16).astype(jnp.float32)
            pieces.append(jnp.concatenate([high, value - high], axis=0).astype(jnp.bfloat16))
        carried = jnp.dot(
            carry, jnp.concatenate(pieces, axis=1), preferred_element_type=jnp.float32
        )
        part = pl.ds(i * width, width)
        grad_ref[:, part] = (local_ref[:, part] + carried).astype(jnp.bfloat16)
        stores.append(
            pltpu.make_async_copy(grad_ref.at[:, part], grad_hbm.at[0, :, part], sems.at[i])
        )
        stores[-1].start()
    own = sum_ref.shape[1] // LANES
    base = lax.axis_index("dp") * own
    for k in range(own):
        sum_ref[:, k * LANES : (k + 1) * LANES] = back_ref[base + k, modes : 2 * modes, :]
    for copy in stores:
        copy.wait()


def to_owners(chunks, owners):
    count, rows, lanes = chunks.shape
    if owners == count:
        return chunks
    narrow = count * lanes // owners
    parts = chunks.reshape(count, rows, lanes // narrow, narrow)
    return jnp.swapaxes(parts, 1, 2).reshape(owners, rows, narrow)


def from_owners(parts, count):
    owners, rows, narrow = parts.shape
    if owners == count:
        return parts
    chunks = parts.reshape(count, owners // count, rows, narrow)
    return jnp.swapaxes(chunks, 1, 2).reshape(count, rows, LANES)


def params(limit=VMEM_LIMIT):
    return pltpu.CompilerParams(vmem_limit_bytes=limit)


def local(batch_count, block_count, grad_out, block_in, residues, decay_rates):
    _, rows, channels = grad_out.shape
    modes = residues.shape[0]
    owners = batch_count * block_count
    chunks = channels // LANES
    anywhere = pl.BlockSpec(memory_space=pl.ANY)
    whole = pl.BlockSpec(memory_space=pltpu.VMEM)
    terms = pl.pallas_call(
        functools.partial(terms_kernel, 2, 256),
        in_specs=[anywhere] * 3,
        out_specs=whole,
        out_shape=jax.ShapeDtypeStruct((chunks, 3 * modes, LANES), jnp.float32),
        scratch_shapes=[
            pltpu.SMEM((modes,), jnp.float32),
            pltpu.VMEM((rows, channels), jnp.bfloat16),
            pltpu.VMEM((rows, channels), jnp.bfloat16),
            pltpu.VMEM((modes * rows // GROUP, 2 * rows), jnp.bfloat16),
            pltpu.VMEM((modes * rows // GROUP, 2 * rows), jnp.bfloat16),
            pltpu.VMEM((GROUP, modes, LANES), jnp.float32),
            pltpu.SemaphoreType.DMA((3, 2)),
        ],
        compiler_params=params(FIRST_LIMIT),
        name="terms",
    )(decay_rates, grad_out, block_in)
    terms = lax.all_to_all(to_owners(terms, owners), ("dp", "seq"), 0, 0)
    local_grad = pl.pallas_call(
        functools.partial(local_grad_kernel, 512),
        in_specs=[anywhere, whole, anywhere],
        out_specs=whole,
        out_shape=jax.ShapeDtypeStruct((rows, channels + 2 * LANES), jnp.float32),
        scratch_shapes=[
            pltpu.SMEM((modes,), jnp.float32),
            pltpu.VMEM((rows, channels), jnp.bfloat16),
            pltpu.VMEM((rows, modes * rows), jnp.bfloat16),
            pltpu.SemaphoreType.DMA((2,)),
        ],
        compiler_params=params(),
        cost_estimate=pl.CostEstimate(
            flops=2 * rows * modes * rows * channels,
            bytes_accessed=6 * rows * channels,
            transcendentals=0,
        ),
        name="local_grad",
    )(decay_rates, residues, grad_out)
    back = pl.pallas_call(
        functools.partial(scan_kernel, batch_count, block_count),
        in_specs=[whole, whole],
        out_specs=whole,
        out_shape=jax.ShapeDtypeStruct((owners, 2 * modes, channels // owners), jnp.float32),
        compiler_params=params(),
        name="scan",
    )(local_grad, terms)
    back = from_owners(lax.all_to_all(back, ("dp", "seq"), 0, 0), chunks)
    return pl.pallas_call(
        functools.partial(finish_kernel, 4),
        in_specs=[whole] * 3,
        out_specs=[anywhere, whole],
        out_shape=[
            jax.ShapeDtypeStruct((1, rows, channels), jnp.bfloat16),
            jax.ShapeDtypeStruct((modes, channels // batch_count), jnp.float32),
        ],
        scratch_shapes=[pltpu.VMEM((rows, channels), jnp.bfloat16), pltpu.SemaphoreType.DMA((4,))],
        compiler_params=params(),
        name="finish",
    )(residues, local_grad, back)


def solution(mesh):
    placed = (P("dp", "seq", None), P("dp", "seq", None), P(), P())
    return jax.shard_map(
        functools.partial(local, mesh.shape["dp"], mesh.shape["seq"]),
        mesh=mesh,
        in_specs=placed,
        out_specs=(P("dp", "seq", None), P(None, "dp")),
        check_vma=False,
    )
```

```python
import functools

import jax
import jax.numpy as jnp
from jax import lax
from jax.experimental import pallas as pl
from jax.experimental.pallas import tpu as pltpu
from jax.sharding import PartitionSpec as P

VMEM_LIMIT = 48 * 1024 * 1024
FIRST_LIMIT = 60 * 1024 * 1024
LANES = 128
SUBLANES = 8
GROUP = 4


def rate_column(rates_ref, mode_count, width):
    rows = lax.broadcasted_iota(jnp.int32, (mode_count, width), 0)
    column = jnp.zeros((mode_count, width), jnp.float32)
    for r in range(mode_count):
        column = jnp.where(rows == r, rates_ref[r], column)
    return column


def mode_gain(rates):
    return jnp.sqrt(1.0 - jnp.exp(-2.0 * rates))


def decay_matrix(rate, rows):
    earlier = lax.broadcasted_iota(jnp.int32, (rows, rows), 0)
    later = lax.broadcasted_iota(jnp.int32, (rows, rows), 1)
    lag = (later - earlier).astype(jnp.float32)
    rates = jnp.full((rows, rows), rate, jnp.float32)
    gain = mode_gain(jnp.full((SUBLANES, rows), rate, jnp.float32))[:1]
    table = gain * jnp.exp(-rates * jnp.maximum(lag, 0.0))
    return jnp.where(lag >= 0.0, table, 0.0).astype(jnp.bfloat16)


def split_bf16(value):
    high = value.astype(jnp.bfloat16)
    return high, (value - high.astype(jnp.float32)).astype(jnp.bfloat16)


def terms_kernel(
    slices,
    sub,
    rates_hbm,
    grad_hbm,
    in_hbm,
    out_ref,
    rates_ref,
    grad_ref,
    in_ref,
    before_ref,
    after_ref,
    lag_ref,
    sems,
):
    modes = rates_ref.shape[0]
    rows, channels = grad_ref.shape
    width = channels // slices
    groups = rows // GROUP
    get_rates = pltpu.make_async_copy(rates_hbm, rates_ref, sems.at[2, 0])
    get_rates.start()
    loads = []
    for i in range(slices):
        part = pl.ds(i * width, width)
        pair = (
            pltpu.make_async_copy(grad_hbm.at[0, :, part], grad_ref.at[:, part], sems.at[0, i]),
            pltpu.make_async_copy(in_hbm.at[0, :, part], in_ref.at[:, part], sems.at[1, i]),
        )
        for copy in pair:
            copy.start()
        loads.append(pair)
    get_rates.wait()
    rates = rate_column(rates_ref, modes, rows)
    gain = mode_gain(rates)
    position = lax.broadcasted_iota(jnp.int32, (modes, rows), 1)
    offset = position.astype(jnp.float32)
    for u in range(1, groups + 1):
        at = slice((u - 1) * modes, u * modes)
        edge = u * GROUP
        before = gain * jnp.exp(-rates * jnp.maximum(edge - offset, 0.0))
        if u < groups:
            after = jnp.exp(-rates * jnp.maximum(offset - edge, 0.0))
            after = jnp.where((position >= edge) & (position < edge + GROUP), after, 0.0)
            high, low = split_bf16(jnp.where(position < edge, before, 0.0))
            after_high, after_low = split_bf16(after)
        else:
            high, low = before.astype(jnp.bfloat16), jnp.zeros((modes, rows), jnp.bfloat16)
            after_high, after_low = jnp.exp(-rates * offset).astype(jnp.bfloat16), low
        before_ref[at, 0:rows] = high
        before_ref[at, rows : 2 * rows] = low
        after_ref[at, 0:rows] = after_high
        after_ref[at, rows : 2 * rows] = after_low
    for k in range(GROUP):
        lag_ref[k] = (gain * jnp.exp(-rates * k))[:, :LANES]

    in_group = lax.broadcasted_iota(jnp.int32, (SUBLANES, sub), 0) % GROUP
    for i in range(slices):
        for copy in loads[i]:
            copy.wait()
        for first in range(i * width, (i + 1) * width, sub):
            part = slice(first, first + sub)
            grad = grad_ref[:, part]
            block = in_ref[:, part]
            twice = jnp.concatenate([block, block], axis=0)
            sums = jnp.dot(before_ref[...], twice, preferred_element_type=jnp.float32)
            twice = jnp.concatenate([grad, grad], axis=0)
            states = jnp.dot(after_ref[...], twice, preferred_element_type=jnp.float32)
            last = slice((groups - 1) * modes, groups * modes)
            carry, state = sums[last], states[last]
            local = sums[0:modes] * states[0:modes]
            for u in range(1, groups - 1):
                at = slice(u * modes, (u + 1) * modes)
                local = local + sums[at] * states[at]
            grad32 = grad.astype(jnp.float32).reshape(rows // SUBLANES, SUBLANES, sub)
            block32 = block.astype(jnp.float32).reshape(rows // SUBLANES, SUBLANES, sub)
            for k in range(GROUP):
                later = pltpu.roll(grad32, SUBLANES - k, 1) if k else grad32
                product = jnp.sum(block32 * later, axis=0)
                if k:
                    product = jnp.where(in_group + k < GROUP, product, 0.0)
                weight = jnp.concatenate([lag_ref[k]] * (sub // LANES), axis=1)
                local = local + weight * jnp.sum(product, axis=0, keepdims=True)
            for k in range(sub // LANES):
                lanes = slice(k * LANES, (k + 1) * LANES)
                chunk = first // LANES + k
                out_ref[chunk, 0:modes, :] = state[:, lanes]
                out_ref[chunk, modes : 2 * modes, :] = carry[:, lanes]
                out_ref[chunk, 2 * modes : 3 * modes, :] = local[:, lanes]


def local_grad_kernel(
    sub, rates_hbm, residues_ref, grad_hbm, out_ref, rates_ref, grad_ref, decay_ref, sems
):
    modes = rates_ref.shape[0]
    rows, channels = grad_ref.shape
    get_rates = pltpu.make_async_copy(rates_hbm, rates_ref, sems.at[0])
    get_rates.start()
    get_grad = pltpu.make_async_copy(grad_hbm.at[0], grad_ref, sems.at[1])
    get_grad.start()
    get_rates.wait()
    for r in range(modes):
        decay_ref[:, r * rows : (r + 1) * rows] = decay_matrix(rates_ref[r], rows)
    column = lax.broadcasted_iota(jnp.int32, (rows, LANES), 1) % modes
    rates = jnp.zeros((rows, LANES), jnp.float32)
    for r in range(modes):
        rates = jnp.where(column == r, rates_ref[r], rates)
    offset = lax.broadcasted_iota(jnp.int32, (rows, LANES), 0).astype(jnp.float32)
    out_ref[:, channels : channels + LANES] = mode_gain(rates) * jnp.exp(-rates * (rows - offset))
    rates = rate_column(rates_ref, modes, LANES)
    out_ref[0:modes, channels + LANES : channels + 2 * LANES] = jnp.exp(-rates * rows)
    get_grad.wait()

    @pl.loop(0, channels // sub)
    def _(i):
        part = pl.ds(pl.multiple_of(i * sub, sub), sub)
        grad32 = grad_ref[:, part].astype(jnp.float32)
        scaled = jnp.concatenate(
            [(grad32 * residues_ref[r : r + 1, part]).astype(jnp.bfloat16) for r in range(modes)],
            axis=0,
        )
        out_ref[:, part] = jnp.dot(decay_ref[...], scaled, preferred_element_type=jnp.float32)


def block_decay(local_ref, modes, width):
    last = local_ref.shape[1] - LANES
    return local_ref[0:modes, last : last + width]


def steps(count, body, start):
    return lax.fori_loop(0, count, body, start, unroll=count <= 8)


def half_kernel(batch_count, half, local_ref, terms_ref, out_ref):
    modes, width = out_ref.shape[1:]
    pieces = terms_ref.shape[0] // (batch_count * half)
    decay = block_decay(local_ref, modes, width)
    zero = jnp.zeros((modes, width), jnp.float32)
    later = lax.axis_index("seq") >= half
    for k in range(pieces):

        def sequence(b, total):
            def state(j, pair):
                total, incoming = pair
                at = (b * half + half - 1 - j) * pieces + k
                weights = terms_ref[at, modes : 2 * modes, :]
                total = total + (terms_ref[at, 2 * modes : 3 * modes, :] + incoming * weights)
                return total, terms_ref[at, 0:modes, :] + decay * incoming

            def weight(j, before):
                return terms_ref[(b * half + j) * pieces + k, modes : 2 * modes, :] + decay * before

            total, incoming = steps(half, state, (total, zero))
            out_ref[b * pieces + k] = jnp.where(later, incoming, steps(half, weight, zero))
            return total

        out_ref[batch_count * pieces + k] = steps(batch_count, sequence, zero)


def scan_kernel(batch_count, half, local_ref, terms_ref, own_ref, other_ref, out_ref):
    modes, width = own_ref.shape[1:]
    pieces = terms_ref.shape[0] // (batch_count * half)
    decay = block_decay(local_ref, modes, width)
    later = lax.axis_index("seq") >= half
    for k in range(pieces):
        last = batch_count * pieces + k
        total = own_ref[last] + other_ref[last]

        def sequence(b, total):
            other = other_ref[b * pieces + k]

            def block(j, incoming):
                at = (b * half + half - 1 - j) * pieces + k
                out_ref[at, 0:modes, :] = incoming
                return terms_ref[at, 0:modes, :] + decay * incoming

            steps(half, block, jnp.where(later, 0.0, other))
            return total + own_ref[b * pieces + k] * other

        total = steps(batch_count, sequence, total)

        def spread(i, carry):
            out_ref[i * pieces + k, modes : 2 * modes, :] = total
            return carry

        lax.fori_loop(0, batch_count * half, spread, 0, unroll=8)


def finish_kernel(slices, residues_ref, local_ref, back_ref, grad_hbm, sum_ref, grad_ref, sems):
    modes, channels = residues_ref.shape
    rows = local_ref.shape[0]
    width = channels // slices
    carry = local_ref[:, channels : channels + 2 * modes].astype(jnp.bfloat16)
    stores = []
    for i in range(slices):
        pieces = []
        for chunk in range(i * width // LANES, (i + 1) * width // LANES):
            lanes = slice(chunk * LANES, (chunk + 1) * LANES)
            value = residues_ref[:, lanes] * back_ref[chunk, 0:modes, :]
            high = value.astype(jnp.bfloat16).astype(jnp.float32)
            pieces.append(jnp.concatenate([high, value - high], axis=0).astype(jnp.bfloat16))
        carried = jnp.dot(
            carry, jnp.concatenate(pieces, axis=1), preferred_element_type=jnp.float32
        )
        part = pl.ds(i * width, width)
        grad_ref[:, part] = (local_ref[:, part] + carried).astype(jnp.bfloat16)
        stores.append(
            pltpu.make_async_copy(grad_ref.at[:, part], grad_hbm.at[0, :, part], sems.at[i])
        )
        stores[-1].start()
    own = sum_ref.shape[1] // LANES
    base = lax.axis_index("dp") * own
    for k in range(own):
        sum_ref[:, k * LANES : (k + 1) * LANES] = back_ref[base + k, modes : 2 * modes, :]
    for copy in stores:
        copy.wait()


def to_owners(chunks, owners):
    count, rows, lanes = chunks.shape
    if owners <= count:
        return chunks.reshape(owners, count // owners * rows, lanes)
    narrow = count * lanes // owners
    parts = chunks.reshape(count, rows, lanes // narrow, narrow)
    return jnp.swapaxes(parts, 1, 2).reshape(owners, rows, narrow)


def from_owners(parts, count):
    owners, rows, narrow = parts.shape
    if owners <= count:
        return parts.reshape(count, owners * rows // count, narrow)
    chunks = parts.reshape(count, owners // count, rows, narrow)
    return jnp.swapaxes(chunks, 1, 2).reshape(count, rows, LANES)


def params(limit=VMEM_LIMIT):
    return pltpu.CompilerParams(vmem_limit_bytes=limit)


def local(batch_count, block_count, grad_out, block_in, residues, decay_rates):
    _, rows, channels = grad_out.shape
    modes = residues.shape[0]
    half = block_count // 2
    owners = batch_count * half
    chunks = channels // LANES
    width = min(LANES, channels // owners)
    pieces = channels // (owners * width)
    groups = [
        [d * block_count + first + j for d in range(batch_count) for j in range(half)]
        for first in (0, half)
    ]

    def exchange(slots):
        return lax.all_to_all(slots, ("dp", "seq"), 0, 0, axis_index_groups=groups)

    anywhere = pl.BlockSpec(memory_space=pl.ANY)
    whole = pl.BlockSpec(memory_space=pltpu.VMEM)
    terms = pl.pallas_call(
        functools.partial(terms_kernel, 2, 256),
        in_specs=[anywhere] * 3,
        out_specs=whole,
        out_shape=jax.ShapeDtypeStruct((chunks, 3 * modes, LANES), jnp.float32),
        scratch_shapes=[
            pltpu.SMEM((modes,), jnp.float32),
            pltpu.VMEM((rows, channels), jnp.bfloat16),
            pltpu.VMEM((rows, channels), jnp.bfloat16),
            pltpu.VMEM((modes * rows // GROUP, 2 * rows), jnp.bfloat16),
            pltpu.VMEM((modes * rows // GROUP, 2 * rows), jnp.bfloat16),
            pltpu.VMEM((GROUP, modes, LANES), jnp.float32),
            pltpu.SemaphoreType.DMA((3, 2)),
        ],
        compiler_params=params(FIRST_LIMIT),
        name="terms",
    )(decay_rates, grad_out, block_in)
    terms = exchange(to_owners(terms, owners)).reshape(owners * pieces, 3 * modes, width)
    local_grad = pl.pallas_call(
        functools.partial(local_grad_kernel, 512),
        in_specs=[anywhere, whole, anywhere],
        out_specs=whole,
        out_shape=jax.ShapeDtypeStruct((rows, channels + 2 * LANES), jnp.float32),
        scratch_shapes=[
            pltpu.SMEM((modes,), jnp.float32),
            pltpu.VMEM((rows, channels), jnp.bfloat16),
            pltpu.VMEM((rows, modes * rows), jnp.bfloat16),
            pltpu.SemaphoreType.DMA((2,)),
        ],
        compiler_params=params(),
        cost_estimate=pl.CostEstimate(
            flops=2 * rows * modes * rows * channels,
            bytes_accessed=6 * rows * channels,
            transcendentals=0,
        ),
        name="local_grad",
    )(decay_rates, residues, grad_out)
    cross = pl.pallas_call(
        functools.partial(half_kernel, batch_count, half),
        in_specs=[whole, whole],
        out_specs=whole,
        out_shape=jax.ShapeDtypeStruct(((batch_count + 1) * pieces, modes, width), jnp.float32),
        compiler_params=params(),
        name="half",
    )(local_grad, terms)
    other = lax.ppermute(cross, "seq", [(s, (s + half) % block_count) for s in range(block_count)])
    back = pl.pallas_call(
        functools.partial(scan_kernel, batch_count, half),
        in_specs=[whole] * 4,
        out_specs=whole,
        out_shape=jax.ShapeDtypeStruct((owners * pieces, 2 * modes, width), jnp.float32),
        compiler_params=params(),
        name="scan",
    )(local_grad, terms, cross, other)
    back = from_owners(exchange(back.reshape(owners, pieces * 2 * modes, width)), chunks)
    return pl.pallas_call(
        functools.partial(finish_kernel, 4),
        in_specs=[whole] * 3,
        out_specs=[anywhere, whole],
        out_shape=[
            jax.ShapeDtypeStruct((1, rows, channels), jnp.bfloat16),
            jax.ShapeDtypeStruct((modes, channels // batch_count), jnp.float32),
        ],
        scratch_shapes=[pltpu.VMEM((rows, channels), jnp.bfloat16), pltpu.SemaphoreType.DMA((4,))],
        compiler_params=params(),
        name="finish",
    )(residues, local_grad, back)


def solution(mesh):
    placed = (P("dp", "seq", None), P("dp", "seq", None), P(), P())
    return jax.shard_map(
        functools.partial(local, mesh.shape["dp"], mesh.shape["seq"]),
        mesh=mesh,
        in_specs=placed,
        out_specs=(P("dp", "seq", None), P(None, "dp")),
        check_vma=False,
    )
```

```python
import functools

import jax
import jax.numpy as jnp
from jax import lax
from jax.experimental import pallas as pl
from jax.experimental.pallas import tpu as pltpu
from jax.sharding import PartitionSpec as P

VMEM_LIMIT = 48 * 1024 * 1024
FIRST_LIMIT = 60 * 1024 * 1024
LANES = 128
SUBLANES = 8
GROUP = 4


def rate_column(rates_ref, mode_count, width):
    rows = lax.broadcasted_iota(jnp.int32, (mode_count, width), 0)
    column = jnp.zeros((mode_count, width), jnp.float32)
    for r in range(mode_count):
        column = jnp.where(rows == r, rates_ref[r], column)
    return column


def mode_gain(rates):
    return jnp.sqrt(1.0 - jnp.exp(-2.0 * rates))


def decay_matrix(rate, rows):
    earlier = lax.broadcasted_iota(jnp.int32, (rows, rows), 0)
    later = lax.broadcasted_iota(jnp.int32, (rows, rows), 1)
    lag = (later - earlier).astype(jnp.float32)
    rates = jnp.full((rows, rows), rate, jnp.float32)
    gain = mode_gain(jnp.full((SUBLANES, rows), rate, jnp.float32))[:1]
    table = gain * jnp.exp(-rates * jnp.maximum(lag, 0.0))
    return jnp.where(lag >= 0.0, table, 0.0).astype(jnp.bfloat16)


def split_bf16(value):
    high = value.astype(jnp.bfloat16)
    return high, (value - high.astype(jnp.float32)).astype(jnp.bfloat16)


def terms_kernel(
    slices,
    sub,
    rates_hbm,
    grad_hbm,
    in_hbm,
    out_ref,
    rates_ref,
    grad_ref,
    in_ref,
    before_ref,
    after_ref,
    lag_ref,
    sems,
    stage_ref,
    out_sems,
):
    modes = rates_ref.shape[0]
    rows, channels = grad_ref.shape
    width = channels // slices
    groups = rows // GROUP
    get_rates = pltpu.make_async_copy(rates_hbm, rates_ref, sems.at[2, 0])
    get_rates.start()
    loads = []
    for i in range(slices):
        part = pl.ds(i * width, width)
        pair = (
            pltpu.make_async_copy(grad_hbm.at[0, :, part], grad_ref.at[:, part], sems.at[0, i]),
            pltpu.make_async_copy(in_hbm.at[0, :, part], in_ref.at[:, part], sems.at[1, i]),
        )
        for copy in pair:
            copy.start()
        loads.append(pair)
    get_rates.wait()
    rates = rate_column(rates_ref, modes, rows)
    gain = mode_gain(rates)
    position = lax.broadcasted_iota(jnp.int32, (modes, rows), 1)
    offset = position.astype(jnp.float32)
    for u in range(1, groups + 1):
        at = slice((u - 1) * modes, u * modes)
        edge = u * GROUP
        before = gain * jnp.exp(-rates * jnp.maximum(edge - offset, 0.0))
        if u < groups:
            after = jnp.exp(-rates * jnp.maximum(offset - edge, 0.0))
            after = jnp.where((position >= edge) & (position < edge + GROUP), after, 0.0)
            high, low = split_bf16(jnp.where(position < edge, before, 0.0))
            after_high, after_low = split_bf16(after)
        else:
            high, low = before.astype(jnp.bfloat16), jnp.zeros((modes, rows), jnp.bfloat16)
            after_high, after_low = jnp.exp(-rates * offset).astype(jnp.bfloat16), low
        before_ref[at, 0:rows] = high
        before_ref[at, rows : 2 * rows] = low
        after_ref[at, 0:rows] = after_high
        after_ref[at, rows : 2 * rows] = after_low
    for k in range(GROUP):
        lag_ref[k] = (gain * jnp.exp(-rates * k))[:, :LANES]

    in_group = lax.broadcasted_iota(jnp.int32, (SUBLANES, sub), 0) % GROUP
    stores = []
    for i in range(slices):
        for copy in loads[i]:
            copy.wait()
        for first in range(i * width, (i + 1) * width, sub):
            part = slice(first, first + sub)
            grad = grad_ref[:, part]
            block = in_ref[:, part]
            twice = jnp.concatenate([block, block], axis=0)
            sums = jnp.dot(before_ref[...], twice, preferred_element_type=jnp.float32)
            twice = jnp.concatenate([grad, grad], axis=0)
            states = jnp.dot(after_ref[...], twice, preferred_element_type=jnp.float32)
            last = slice((groups - 1) * modes, groups * modes)
            carry, state = sums[last], states[last]
            local = sums[0:modes] * states[0:modes]
            for u in range(1, groups - 1):
                at = slice(u * modes, (u + 1) * modes)
                local = local + sums[at] * states[at]
            grad32 = grad.astype(jnp.float32).reshape(rows // SUBLANES, SUBLANES, sub)
            block32 = block.astype(jnp.float32).reshape(rows // SUBLANES, SUBLANES, sub)
            for k in range(GROUP):
                later = pltpu.roll(grad32, SUBLANES - k, 1) if k else grad32
                product = jnp.sum(block32 * later, axis=0)
                if k:
                    product = jnp.where(in_group + k < GROUP, product, 0.0)
                weight = jnp.concatenate([lag_ref[k]] * (sub // LANES), axis=1)
                local = local + weight * jnp.sum(product, axis=0, keepdims=True)
            for k in range(sub // LANES):
                lanes = slice(k * LANES, (k + 1) * LANES)
                chunk = first // LANES + k
                stage_ref[chunk, 0:modes, :] = state[:, lanes]
                stage_ref[chunk, modes : 2 * modes, :] = carry[:, lanes]
                stage_ref[chunk, 2 * modes : 3 * modes, :] = local[:, lanes]
        span = pl.ds(i * width // LANES, width // LANES)
        stores.append(pltpu.make_async_copy(stage_ref.at[span], out_ref.at[span], out_sems.at[i]))
        stores[-1].start()
    for copy in stores:
        copy.wait()


def local_grad_kernel(
    sub, rates_hbm, residues_ref, grad_hbm, out_ref, rates_ref, grad_ref, decay_ref, sems
):
    modes = rates_ref.shape[0]
    rows, channels = grad_ref.shape
    get_rates = pltpu.make_async_copy(rates_hbm, rates_ref, sems.at[0])
    get_rates.start()
    get_grad = pltpu.make_async_copy(grad_hbm.at[0], grad_ref, sems.at[1])
    get_grad.start()
    get_rates.wait()
    for r in range(modes):
        decay_ref[:, r * rows : (r + 1) * rows] = decay_matrix(rates_ref[r], rows)
    column = lax.broadcasted_iota(jnp.int32, (rows, LANES), 1) % modes
    rates = jnp.zeros((rows, LANES), jnp.float32)
    for r in range(modes):
        rates = jnp.where(column == r, rates_ref[r], rates)
    offset = lax.broadcasted_iota(jnp.int32, (rows, LANES), 0).astype(jnp.float32)
    out_ref[:, channels : channels + LANES] = mode_gain(rates) * jnp.exp(-rates * (rows - offset))
    rates = rate_column(rates_ref, modes, LANES)
    out_ref[0:modes, channels + LANES : channels + 2 * LANES] = jnp.exp(-rates * rows)
    get_grad.wait()

    @pl.loop(0, channels // sub)
    def _(i):
        part = pl.ds(pl.multiple_of(i * sub, sub), sub)
        grad32 = grad_ref[:, part].astype(jnp.float32)
        scaled = jnp.concatenate(
            [(grad32 * residues_ref[r : r + 1, part]).astype(jnp.bfloat16) for r in range(modes)],
            axis=0,
        )
        out_ref[:, part] = jnp.dot(decay_ref[...], scaled, preferred_element_type=jnp.float32)


def block_decay(local_ref, modes, width):
    last = local_ref.shape[1] - LANES
    return local_ref[0:modes, last : last + width]


def steps(count, body, start):
    return lax.fori_loop(0, count, body, start, unroll=count <= 8)


def half_kernel(batch_count, half, local_ref, terms_ref, out_ref):
    modes, width = out_ref.shape[1:]
    pieces = terms_ref.shape[0] // (batch_count * half)
    decay = block_decay(local_ref, modes, width)
    zero = jnp.zeros((modes, width), jnp.float32)
    later = lax.axis_index("seq") >= half
    for k in range(pieces):

        def sequence(b, total):
            def state(j, pair):
                total, incoming = pair
                at = (b * half + half - 1 - j) * pieces + k
                weights = terms_ref[at, modes : 2 * modes, :]
                total = total + (terms_ref[at, 2 * modes : 3 * modes, :] + incoming * weights)
                return total, terms_ref[at, 0:modes, :] + decay * incoming

            def weight(j, before):
                return terms_ref[(b * half + j) * pieces + k, modes : 2 * modes, :] + decay * before

            total, incoming = steps(half, state, (total, zero))
            out_ref[b * pieces + k] = jnp.where(later, incoming, steps(half, weight, zero))
            return total

        out_ref[batch_count * pieces + k] = steps(batch_count, sequence, zero)


def scan_kernel(batch_count, half, local_ref, terms_ref, own_ref, other_ref, out_ref):
    modes, width = own_ref.shape[1:]
    pieces = terms_ref.shape[0] // (batch_count * half)
    decay = block_decay(local_ref, modes, width)
    later = lax.axis_index("seq") >= half
    for k in range(pieces):
        last = batch_count * pieces + k
        total = own_ref[last] + other_ref[last]

        def sequence(b, total):
            other = other_ref[b * pieces + k]

            def block(j, incoming):
                at = (b * half + half - 1 - j) * pieces + k
                out_ref[at, 0:modes, :] = incoming
                return terms_ref[at, 0:modes, :] + decay * incoming

            steps(half, block, jnp.where(later, 0.0, other))
            return total + own_ref[b * pieces + k] * other

        total = steps(batch_count, sequence, total)

        def spread(i, carry):
            out_ref[i * pieces + k, modes : 2 * modes, :] = total
            return carry

        lax.fori_loop(0, batch_count * half, spread, 0, unroll=8)


def finish_kernel(slices, residues_ref, local_ref, back_ref, grad_hbm, sum_hbm, grad_ref, sum_ref, sems):
    modes, channels = residues_ref.shape
    rows = local_ref.shape[0]
    width = channels // slices
    carry = local_ref[:, channels : channels + 2 * modes].astype(jnp.bfloat16)
    own = sum_ref.shape[1] // LANES
    base = lax.axis_index("dp") * own
    for k in range(own):
        sum_ref[:, k * LANES : (k + 1) * LANES] = back_ref[base + k, modes : 2 * modes, :]
    stores = [pltpu.make_async_copy(sum_ref, sum_hbm, sems.at[slices])]
    stores[0].start()
    for i in range(slices):
        pieces = []
        for chunk in range(i * width // LANES, (i + 1) * width // LANES):
            lanes = slice(chunk * LANES, (chunk + 1) * LANES)
            value = residues_ref[:, lanes] * back_ref[chunk, 0:modes, :]
            high = value.astype(jnp.bfloat16).astype(jnp.float32)
            pieces.append(jnp.concatenate([high, value - high], axis=0).astype(jnp.bfloat16))
        carried = jnp.dot(
            carry, jnp.concatenate(pieces, axis=1), preferred_element_type=jnp.float32
        )
        part = pl.ds(i * width, width)
        grad_ref[:, part] = (local_ref[:, part] + carried).astype(jnp.bfloat16)
        stores.append(
            pltpu.make_async_copy(grad_ref.at[:, part], grad_hbm.at[0, :, part], sems.at[i])
        )
        stores[-1].start()
    for copy in stores:
        copy.wait()


def to_owners(chunks, owners):
    count, rows, lanes = chunks.shape
    if owners <= count:
        return chunks.reshape(owners, count // owners * rows, lanes)
    narrow = count * lanes // owners
    parts = chunks.reshape(count, rows, lanes // narrow, narrow)
    return jnp.swapaxes(parts, 1, 2).reshape(owners, rows, narrow)


def from_owners(parts, count):
    owners, rows, narrow = parts.shape
    if owners <= count:
        return parts.reshape(count, owners * rows // count, narrow)
    chunks = parts.reshape(count, owners // count, rows, narrow)
    return jnp.swapaxes(chunks, 1, 2).reshape(count, rows, LANES)


def params(limit=VMEM_LIMIT):
    return pltpu.CompilerParams(vmem_limit_bytes=limit)


def local(batch_count, block_count, grad_out, block_in, residues, decay_rates):
    _, rows, channels = grad_out.shape
    modes = residues.shape[0]
    half = block_count // 2
    owners = batch_count * half
    chunks = channels // LANES
    width = min(LANES, channels // owners)
    pieces = channels // (owners * width)
    groups = [
        [d * block_count + first + j for d in range(batch_count) for j in range(half)]
        for first in (0, half)
    ]

    def exchange(slots):
        return lax.all_to_all(slots, ("dp", "seq"), 0, 0, axis_index_groups=groups)

    anywhere = pl.BlockSpec(memory_space=pl.ANY)
    whole = pl.BlockSpec(memory_space=pltpu.VMEM)
    terms = pl.pallas_call(
        functools.partial(terms_kernel, 2, 256),
        in_specs=[anywhere] * 3,
        out_specs=anywhere,
        out_shape=jax.ShapeDtypeStruct((chunks, 3 * modes, LANES), jnp.float32),
        scratch_shapes=[
            pltpu.SMEM((modes,), jnp.float32),
            pltpu.VMEM((rows, channels), jnp.bfloat16),
            pltpu.VMEM((rows, channels), jnp.bfloat16),
            pltpu.VMEM((modes * rows // GROUP, 2 * rows), jnp.bfloat16),
            pltpu.VMEM((modes * rows // GROUP, 2 * rows), jnp.bfloat16),
            pltpu.VMEM((GROUP, modes, LANES), jnp.float32),
            pltpu.SemaphoreType.DMA((3, 2)),
            pltpu.VMEM((chunks, 3 * modes, LANES), jnp.float32),
            pltpu.SemaphoreType.DMA((2,)),
        ],
        compiler_params=params(FIRST_LIMIT),
        name="terms",
    )(decay_rates, grad_out, block_in)
    terms = exchange(to_owners(terms, owners)).reshape(owners * pieces, 3 * modes, width)
    local_grad = pl.pallas_call(
        functools.partial(local_grad_kernel, 512),
        in_specs=[anywhere, whole, anywhere],
        out_specs=whole,
        out_shape=jax.ShapeDtypeStruct((rows, channels + 2 * LANES), jnp.float32),
        scratch_shapes=[
            pltpu.SMEM((modes,), jnp.float32),
            pltpu.VMEM((rows, channels), jnp.bfloat16),
            pltpu.VMEM((rows, modes * rows), jnp.bfloat16),
            pltpu.SemaphoreType.DMA((2,)),
        ],
        compiler_params=params(),
        cost_estimate=pl.CostEstimate(
            flops=2 * rows * modes * rows * channels,
            bytes_accessed=6 * rows * channels,
            transcendentals=0,
        ),
        name="local_grad",
    )(decay_rates, residues, grad_out)
    cross = pl.pallas_call(
        functools.partial(half_kernel, batch_count, half),
        in_specs=[whole, whole],
        out_specs=whole,
        out_shape=jax.ShapeDtypeStruct(((batch_count + 1) * pieces, modes, width), jnp.float32),
        compiler_params=params(),
        name="half",
    )(local_grad, terms)
    other = lax.ppermute(cross, "seq", [(s, (s + half) % block_count) for s in range(block_count)])
    back = pl.pallas_call(
        functools.partial(scan_kernel, batch_count, half),
        in_specs=[whole] * 4,
        out_specs=whole,
        out_shape=jax.ShapeDtypeStruct((owners * pieces, 2 * modes, width), jnp.float32),
        compiler_params=params(),
        name="scan",
    )(local_grad, terms, cross, other)
    back = from_owners(exchange(back.reshape(owners, pieces * 2 * modes, width)), chunks)
    return pl.pallas_call(
        functools.partial(finish_kernel, 4),
        in_specs=[whole] * 3,
        out_specs=[anywhere, anywhere],
        out_shape=[
            jax.ShapeDtypeStruct((1, rows, channels), jnp.bfloat16),
            jax.ShapeDtypeStruct((modes, channels // batch_count), jnp.float32),
        ],
        scratch_shapes=[
            pltpu.VMEM((rows, channels), jnp.bfloat16),
            pltpu.VMEM((modes, channels // batch_count), jnp.float32),
            pltpu.SemaphoreType.DMA((5,)),
        ],
        compiler_params=params(),
        name="finish",
    )(residues, local_grad, back)


def solution(mesh):
    placed = (P("dp", "seq", None), P("dp", "seq", None), P(), P())
    return jax.shard_map(
        functools.partial(local, mesh.shape["dp"], mesh.shape["seq"]),
        mesh=mesh,
        in_specs=placed,
        out_specs=(P("dp", "seq", None), P(None, "dp")),
        check_vma=False,
    )
```

```python
import functools

import jax
import jax.numpy as jnp
from jax import lax
from jax.experimental import pallas as pl
from jax.experimental.pallas import tpu as pltpu
from jax.sharding import PartitionSpec as P

VMEM_LIMIT = 48 * 1024 * 1024
FIRST_LIMIT = 60 * 1024 * 1024
LANES = 128
SUBLANES = 8
GROUP = 4


def rate_column(rates_ref, mode_count, width):
    rows = lax.broadcasted_iota(jnp.int32, (mode_count, width), 0)
    column = jnp.zeros((mode_count, width), jnp.float32)
    for r in range(mode_count):
        column = jnp.where(rows == r, rates_ref[r], column)
    return column


def mode_gain(rates):
    return jnp.sqrt(1.0 - jnp.exp(-2.0 * rates))


def decay_matrix(rate, rows):
    earlier = lax.broadcasted_iota(jnp.int32, (rows, rows), 0)
    later = lax.broadcasted_iota(jnp.int32, (rows, rows), 1)
    lag = (later - earlier).astype(jnp.float32)
    rates = jnp.full((rows, rows), rate, jnp.float32)
    gain = mode_gain(jnp.full((SUBLANES, rows), rate, jnp.float32))[:1]
    table = gain * jnp.exp(-rates * jnp.maximum(lag, 0.0))
    return jnp.where(lag >= 0.0, table, 0.0).astype(jnp.bfloat16)


def split_bf16(value):
    high = value.astype(jnp.bfloat16)
    return high, (value - high.astype(jnp.float32)).astype(jnp.bfloat16)


def terms_kernel(
    slices,
    sub,
    slot,
    rates_hbm,
    grad_hbm,
    in_hbm,
    out_ref,
    rates_ref,
    grad_ref,
    in_ref,
    before_ref,
    after_ref,
    lag_ref,
    sems,
    stage_ref,
    out_sems,
):
    modes = rates_ref.shape[0]
    rows, channels = grad_ref.shape
    width = channels // slices
    groups = rows // GROUP
    get_rates = pltpu.make_async_copy(rates_hbm, rates_ref, sems.at[2, 0])
    get_rates.start()
    loads = []
    for i in range(slices):
        part = pl.ds(i * width, width)
        pair = (
            pltpu.make_async_copy(grad_hbm.at[0, :, part], grad_ref.at[:, part], sems.at[0, i]),
            pltpu.make_async_copy(in_hbm.at[0, :, part], in_ref.at[:, part], sems.at[1, i]),
        )
        for copy in pair:
            copy.start()
        loads.append(pair)
    get_rates.wait()
    rates = rate_column(rates_ref, modes, rows)
    gain = mode_gain(rates)
    position = lax.broadcasted_iota(jnp.int32, (modes, rows), 1)
    offset = position.astype(jnp.float32)
    for u in range(1, groups + 1):
        at = slice((u - 1) * modes, u * modes)
        edge = u * GROUP
        before = gain * jnp.exp(-rates * jnp.maximum(edge - offset, 0.0))
        if u < groups:
            after = jnp.exp(-rates * jnp.maximum(offset - edge, 0.0))
            after = jnp.where((position >= edge) & (position < edge + GROUP), after, 0.0)
            high, low = split_bf16(jnp.where(position < edge, before, 0.0))
            after_high, after_low = split_bf16(after)
        else:
            high, low = before.astype(jnp.bfloat16), jnp.zeros((modes, rows), jnp.bfloat16)
            after_high, after_low = jnp.exp(-rates * offset).astype(jnp.bfloat16), low
        before_ref[at, 0:rows] = high
        before_ref[at, rows : 2 * rows] = low
        after_ref[at, 0:rows] = after_high
        after_ref[at, rows : 2 * rows] = after_low
    for k in range(GROUP):
        lag_ref[k] = (gain * jnp.exp(-rates * k))[:, :LANES]

    in_group = lax.broadcasted_iota(jnp.int32, (SUBLANES, sub), 0) % GROUP
    stores = []
    for i in range(slices):
        for copy in loads[i]:
            copy.wait()
        for first in range(i * width, (i + 1) * width, sub):
            part = slice(first, first + sub)
            grad = grad_ref[:, part]
            block = in_ref[:, part]
            twice = jnp.concatenate([block, block], axis=0)
            sums = jnp.dot(before_ref[...], twice, preferred_element_type=jnp.float32)
            twice = jnp.concatenate([grad, grad], axis=0)
            states = jnp.dot(after_ref[...], twice, preferred_element_type=jnp.float32)
            last = slice((groups - 1) * modes, groups * modes)
            carry, state = sums[last], states[last]
            local = sums[0:modes] * states[0:modes]
            for u in range(1, groups - 1):
                at = slice(u * modes, (u + 1) * modes)
                local = local + sums[at] * states[at]
            grad32 = grad.astype(jnp.float32).reshape(rows // SUBLANES, SUBLANES, sub)
            block32 = block.astype(jnp.float32).reshape(rows // SUBLANES, SUBLANES, sub)
            for k in range(GROUP):
                later = pltpu.roll(grad32, SUBLANES - k, 1) if k else grad32
                product = jnp.sum(block32 * later, axis=0)
                if k:
                    product = jnp.where(in_group + k < GROUP, product, 0.0)
                weight = jnp.concatenate([lag_ref[k]] * (sub // LANES), axis=1)
                local = local + weight * jnp.sum(product, axis=0, keepdims=True)
            for k in range(sub // LANES):
                lanes = slice(k * LANES, (k + 1) * LANES)
                chunk = slot(first // LANES + k)
                stage_ref[chunk, 0:modes, :] = state[:, lanes]
                stage_ref[chunk, modes : 2 * modes, :] = carry[:, lanes]
                stage_ref[chunk, 2 * modes : 3 * modes, :] = local[:, lanes]
        chunks = [slot(chunk) for chunk in range(i * width // LANES, (i + 1) * width // LANES)]
        span = pl.ds(min(chunks), len(chunks))
        stores.append(pltpu.make_async_copy(stage_ref.at[span], out_ref.at[span], out_sems.at[i]))
        stores[-1].start()
    for copy in stores:
        copy.wait()


def local_grad_kernel(
    sub, rates_hbm, residues_ref, grad_hbm, out_ref, rates_ref, grad_ref, decay_ref, sems
):
    modes = rates_ref.shape[0]
    rows, channels = grad_ref.shape
    get_rates = pltpu.make_async_copy(rates_hbm, rates_ref, sems.at[0])
    get_rates.start()
    get_grad = pltpu.make_async_copy(grad_hbm.at[0], grad_ref, sems.at[1])
    get_grad.start()
    get_rates.wait()
    for r in range(modes):
        decay_ref[:, r * rows : (r + 1) * rows] = decay_matrix(rates_ref[r], rows)
    column = lax.broadcasted_iota(jnp.int32, (rows, LANES), 1) % modes
    rates = jnp.zeros((rows, LANES), jnp.float32)
    for r in range(modes):
        rates = jnp.where(column == r, rates_ref[r], rates)
    offset = lax.broadcasted_iota(jnp.int32, (rows, LANES), 0).astype(jnp.float32)
    out_ref[:, channels : channels + LANES] = mode_gain(rates) * jnp.exp(-rates * (rows - offset))
    rates = rate_column(rates_ref, modes, LANES)
    out_ref[0:modes, channels + LANES : channels + 2 * LANES] = jnp.exp(-rates * rows)
    get_grad.wait()

    @pl.loop(0, channels // sub)
    def _(i):
        part = pl.ds(pl.multiple_of(i * sub, sub), sub)
        grad32 = grad_ref[:, part].astype(jnp.float32)
        scaled = jnp.concatenate(
            [(grad32 * residues_ref[r : r + 1, part]).astype(jnp.bfloat16) for r in range(modes)],
            axis=0,
        )
        out_ref[:, part] = jnp.dot(decay_ref[...], scaled, preferred_element_type=jnp.float32)


def block_decay(local_ref, modes, width):
    last = local_ref.shape[1] - LANES
    return local_ref[0:modes, last : last + width]


def steps(count, body, start):
    return lax.fori_loop(0, count, body, start, unroll=count <= 8)


def half_kernel(batch_count, half, mask, local_ref, terms_ref, out_ref):
    modes, width = out_ref.shape[1:]
    pieces = terms_ref.shape[0] // (batch_count * half)
    decay = block_decay(local_ref, modes, width)
    zero = jnp.zeros((modes, width), jnp.float32)
    later = lax.axis_index("seq") >= half
    for k in range(pieces):

        def sequence(b, total):
            def state(j, pair):
                total, incoming = pair
                at = ((b * half + half - 1 - j) ^ mask) * pieces + k
                weights = terms_ref[at, modes : 2 * modes, :]
                total = total + (terms_ref[at, 2 * modes : 3 * modes, :] + incoming * weights)
                return total, terms_ref[at, 0:modes, :] + decay * incoming

            def weight(j, before):
                return terms_ref[((b * half + j) ^ mask) * pieces + k, modes : 2 * modes, :] + decay * before

            total, incoming = steps(half, state, (total, zero))
            out_ref[b * pieces + k] = jnp.where(later, incoming, steps(half, weight, zero))
            return total

        out_ref[batch_count * pieces + k] = steps(batch_count, sequence, zero)


def scan_kernel(batch_count, half, mask, local_ref, terms_ref, own_ref, other_ref, out_ref):
    modes, width = own_ref.shape[1:]
    pieces = terms_ref.shape[0] // (batch_count * half)
    decay = block_decay(local_ref, modes, width)
    later = lax.axis_index("seq") >= half
    for k in range(pieces):
        last = batch_count * pieces + k
        total = own_ref[last] + other_ref[last]

        def sequence(b, total):
            other = other_ref[b * pieces + k]

            def block(j, incoming):
                at = ((b * half + half - 1 - j) ^ mask) * pieces + k
                out_ref[at, 0:modes, :] = incoming
                return terms_ref[at, 0:modes, :] + decay * incoming

            steps(half, block, jnp.where(later, 0.0, other))
            return total + own_ref[b * pieces + k] * other

        total = steps(batch_count, sequence, total)

        def spread(i, carry):
            out_ref[i * pieces + k, modes : 2 * modes, :] = total
            return carry

        lax.fori_loop(0, batch_count * half, spread, 0, unroll=8)


def finish_kernel(slices, slot, residues_ref, local_ref, back_ref, grad_hbm, sum_hbm, grad_ref, sum_ref, sems):
    modes, channels = residues_ref.shape
    rows = local_ref.shape[0]
    width = channels // slices
    carry = local_ref[:, channels : channels + 2 * modes].astype(jnp.bfloat16)
    own = sum_ref.shape[1] // LANES
    base = lax.axis_index("dp") * own
    for k in range(own):
        sum_ref[:, k * LANES : (k + 1) * LANES] = back_ref[slot(base + k), modes : 2 * modes, :]
    stores = [pltpu.make_async_copy(sum_ref, sum_hbm, sems.at[slices])]
    stores[0].start()
    for i in range(slices):
        pieces = []
        for chunk in range(i * width // LANES, (i + 1) * width // LANES):
            lanes = slice(chunk * LANES, (chunk + 1) * LANES)
            value = residues_ref[:, lanes] * back_ref[slot(chunk), 0:modes, :]
            high = value.astype(jnp.bfloat16).astype(jnp.float32)
            pieces.append(jnp.concatenate([high, value - high], axis=0).astype(jnp.bfloat16))
        carried = jnp.dot(
            carry, jnp.concatenate(pieces, axis=1), preferred_element_type=jnp.float32
        )
        part = pl.ds(i * width, width)
        grad_ref[:, part] = (local_ref[:, part] + carried).astype(jnp.bfloat16)
        stores.append(
            pltpu.make_async_copy(grad_ref.at[:, part], grad_hbm.at[0, :, part], sems.at[i])
        )
        stores[-1].start()
    for copy in stores:
        copy.wait()


def to_owners(chunks, owners):
    count, rows, lanes = chunks.shape
    if owners <= count:
        return chunks.reshape(owners, count // owners * rows, lanes)
    narrow = count * lanes // owners
    parts = chunks.reshape(count, rows, lanes // narrow, narrow)
    return jnp.swapaxes(parts, 1, 2).reshape(owners, rows, narrow)


def from_owners(parts, count):
    owners, rows, narrow = parts.shape
    if owners <= count:
        return parts.reshape(count, owners * rows // count, narrow)
    chunks = parts.reshape(count, owners // count, rows, narrow)
    return jnp.swapaxes(chunks, 1, 2).reshape(count, rows, LANES)


def params(limit=VMEM_LIMIT):
    return pltpu.CompilerParams(vmem_limit_bytes=limit)


def local(batch_count, block_count, grad_out, block_in, residues, decay_rates):
    _, rows, channels = grad_out.shape
    modes = residues.shape[0]
    half = block_count // 2
    owners = batch_count * half
    chunks = channels // LANES
    width = min(LANES, channels // owners)
    pieces = channels // (owners * width)
    anywhere = pl.BlockSpec(memory_space=pl.ANY)
    whole = pl.BlockSpec(memory_space=pltpu.VMEM)
    mask = (batch_count - 1) * half + 1 if half > 1 and owners & (owners - 1) == 0 else 0

    def exchange(slots):
        places = [d * block_count + j for d in range(batch_count) for j in range(half)]
        groups = [[first + places[p ^ mask] for p in range(owners)] for first in (0, half)]
        return lax.all_to_all(slots, ("dp", "seq"), 0, 0, axis_index_groups=groups)

    def slot(chunk):
        if owners > chunks:
            return chunk
        share = chunks // owners
        return ((chunk // share) ^ mask) * share + chunk % share

    def reorder(slots):
        if owners <= chunks:
            return slots
        return slots[jnp.array([p ^ mask for p in range(owners)])]

    terms = pl.pallas_call(
        functools.partial(terms_kernel, 2, 256, slot),
        in_specs=[anywhere] * 3,
        out_specs=anywhere,
        out_shape=jax.ShapeDtypeStruct((chunks, 3 * modes, LANES), jnp.float32),
        scratch_shapes=[
            pltpu.SMEM((modes,), jnp.float32),
            pltpu.VMEM((rows, channels), jnp.bfloat16),
            pltpu.VMEM((rows, channels), jnp.bfloat16),
            pltpu.VMEM((modes * rows // GROUP, 2 * rows), jnp.bfloat16),
            pltpu.VMEM((modes * rows // GROUP, 2 * rows), jnp.bfloat16),
            pltpu.VMEM((GROUP, modes, LANES), jnp.float32),
            pltpu.SemaphoreType.DMA((3, 2)),
            pltpu.VMEM((chunks, 3 * modes, LANES), jnp.float32),
            pltpu.SemaphoreType.DMA((2,)),
        ],
        compiler_params=params(FIRST_LIMIT),
        name="terms",
    )(decay_rates, grad_out, block_in)
    terms = exchange(reorder(to_owners(terms, owners)))
    terms = terms.reshape(owners * pieces, 3 * modes, width)
    local_grad = pl.pallas_call(
        functools.partial(local_grad_kernel, 512),
        in_specs=[anywhere, whole, anywhere],
        out_specs=whole,
        out_shape=jax.ShapeDtypeStruct((rows, channels + 2 * LANES), jnp.float32),
        scratch_shapes=[
            pltpu.SMEM((modes,), jnp.float32),
            pltpu.VMEM((rows, channels), jnp.bfloat16),
            pltpu.VMEM((rows, modes * rows), jnp.bfloat16),
            pltpu.SemaphoreType.DMA((2,)),
        ],
        compiler_params=params(),
        cost_estimate=pl.CostEstimate(
            flops=2 * rows * modes * rows * channels,
            bytes_accessed=6 * rows * channels,
            transcendentals=0,
        ),
        name="local_grad",
    )(decay_rates, residues, grad_out)
    cross = pl.pallas_call(
        functools.partial(half_kernel, batch_count, half, mask),
        in_specs=[whole, whole],
        out_specs=whole,
        out_shape=jax.ShapeDtypeStruct(((batch_count + 1) * pieces, modes, width), jnp.float32),
        compiler_params=params(),
        name="half",
    )(local_grad, terms)
    other = lax.ppermute(cross, "seq", [(s, (s + half) % block_count) for s in range(block_count)])
    back = pl.pallas_call(
        functools.partial(scan_kernel, batch_count, half, mask),
        in_specs=[whole] * 4,
        out_specs=whole,
        out_shape=jax.ShapeDtypeStruct((owners * pieces, 2 * modes, width), jnp.float32),
        compiler_params=params(),
        name="scan",
    )(local_grad, terms, cross, other)
    back = exchange(back.reshape(owners, pieces * 2 * modes, width))
    back = from_owners(reorder(back), chunks)
    return pl.pallas_call(
        functools.partial(finish_kernel, 4, slot),
        in_specs=[whole] * 3,
        out_specs=[anywhere, anywhere],
        out_shape=[
            jax.ShapeDtypeStruct((1, rows, channels), jnp.bfloat16),
            jax.ShapeDtypeStruct((modes, channels // batch_count), jnp.float32),
        ],
        scratch_shapes=[
            pltpu.VMEM((rows, channels), jnp.bfloat16),
            pltpu.VMEM((modes, channels // batch_count), jnp.float32),
            pltpu.SemaphoreType.DMA((5,)),
        ],
        compiler_params=params(),
        name="finish",
    )(residues, local_grad, back)


def solution(mesh):
    placed = (P("dp", "seq", None), P("dp", "seq", None), P(), P())
    return jax.shard_map(
        functools.partial(local, mesh.shape["dp"], mesh.shape["seq"]),
        mesh=mesh,
        in_specs=placed,
        out_specs=(P("dp", "seq", None), P(None, "dp")),
        check_vma=False,
    )
```

```python
import functools

import jax
import jax.numpy as jnp
from jax import lax
from jax.experimental import pallas as pl
from jax.experimental.pallas import tpu as pltpu
from jax.sharding import PartitionSpec as P

VMEM_LIMIT = 48 * 1024 * 1024
FIRST_LIMIT = 60 * 1024 * 1024
LANES = 128
SUBLANES = 8
GROUP = 4


def rate_column(rates_ref, mode_count, width):
    rows = lax.broadcasted_iota(jnp.int32, (mode_count, width), 0)
    column = jnp.zeros((mode_count, width), jnp.float32)
    for r in range(mode_count):
        column = jnp.where(rows == r, rates_ref[r], column)
    return column


def mode_gain(rates):
    return jnp.sqrt(1.0 - jnp.exp(-2.0 * rates))


def decay_matrix(rate, rows):
    earlier = lax.broadcasted_iota(jnp.int32, (rows, rows), 0)
    later = lax.broadcasted_iota(jnp.int32, (rows, rows), 1)
    lag = (later - earlier).astype(jnp.float32)
    rates = jnp.full((rows, rows), rate, jnp.float32)
    gain = mode_gain(jnp.full((SUBLANES, rows), rate, jnp.float32))[:1]
    table = gain * jnp.exp(-rates * jnp.maximum(lag, 0.0))
    return jnp.where(lag >= 0.0, table, 0.0).astype(jnp.bfloat16)


def split_bf16(value):
    high = value.astype(jnp.bfloat16)
    return high, (value - high.astype(jnp.float32)).astype(jnp.bfloat16)


def terms_kernel(
    slices,
    sub,
    places,
    rates_hbm,
    grad_hbm,
    in_hbm,
    out_ref,
    rates_ref,
    grad_ref,
    in_ref,
    before_ref,
    after_ref,
    lag_ref,
    sems,
    stage_ref,
    out_sems,
):
    modes = rates_ref.shape[0]
    rows, channels = grad_ref.shape
    width = channels // slices
    groups = rows // GROUP
    get_rates = pltpu.make_async_copy(rates_hbm, rates_ref, sems.at[2, 0])
    get_rates.start()
    loads = []
    for i in range(slices):
        part = pl.ds(i * width, width)
        pair = (
            pltpu.make_async_copy(grad_hbm.at[0, :, part], grad_ref.at[:, part], sems.at[0, i]),
            pltpu.make_async_copy(in_hbm.at[0, :, part], in_ref.at[:, part], sems.at[1, i]),
        )
        for copy in pair:
            copy.start()
        loads.append(pair)
    get_rates.wait()
    rates = rate_column(rates_ref, modes, rows)
    gain = mode_gain(rates)
    position = lax.broadcasted_iota(jnp.int32, (modes, rows), 1)
    offset = position.astype(jnp.float32)
    for u in range(1, groups + 1):
        at = slice((u - 1) * modes, u * modes)
        edge = u * GROUP
        before = gain * jnp.exp(-rates * jnp.maximum(edge - offset, 0.0))
        if u < groups:
            after = jnp.exp(-rates * jnp.maximum(offset - edge, 0.0))
            after = jnp.where((position >= edge) & (position < edge + GROUP), after, 0.0)
            high, low = split_bf16(jnp.where(position < edge, before, 0.0))
            after_high, after_low = split_bf16(after)
        else:
            high, low = before.astype(jnp.bfloat16), jnp.zeros((modes, rows), jnp.bfloat16)
            after_high, after_low = jnp.exp(-rates * offset).astype(jnp.bfloat16), low
        before_ref[at, 0:rows] = high
        before_ref[at, rows : 2 * rows] = low
        after_ref[at, 0:rows] = after_high
        after_ref[at, rows : 2 * rows] = after_low
    for k in range(GROUP):
        lag_ref[k] = (gain * jnp.exp(-rates * k))[:, :LANES]

    in_group = lax.broadcasted_iota(jnp.int32, (SUBLANES, sub), 0) % GROUP
    stores = []
    for i in range(slices):
        for copy in loads[i]:
            copy.wait()
        for first in range(i * width, (i + 1) * width, sub):
            part = slice(first, first + sub)
            grad = grad_ref[:, part]
            block = in_ref[:, part]
            twice = jnp.concatenate([block, block], axis=0)
            sums = jnp.dot(before_ref[...], twice, preferred_element_type=jnp.float32)
            twice = jnp.concatenate([grad, grad], axis=0)
            states = jnp.dot(after_ref[...], twice, preferred_element_type=jnp.float32)
            last = slice((groups - 1) * modes, groups * modes)
            carry, state = sums[last], states[last]
            local = sums[0:modes] * states[0:modes]
            for u in range(1, groups - 1):
                at = slice(u * modes, (u + 1) * modes)
                local = local + sums[at] * states[at]
            grad32 = grad.astype(jnp.float32).reshape(rows // SUBLANES, SUBLANES, sub)
            block32 = block.astype(jnp.float32).reshape(rows // SUBLANES, SUBLANES, sub)
            for k in range(GROUP):
                later = pltpu.roll(grad32, SUBLANES - k, 1) if k else grad32
                product = jnp.sum(block32 * later, axis=0)
                if k:
                    product = jnp.where(in_group + k < GROUP, product, 0.0)
                weight = jnp.concatenate([lag_ref[k]] * (sub // LANES), axis=1)
                local = local + weight * jnp.sum(product, axis=0, keepdims=True)
            for k in range(sub // LANES):
                for low, high, at in places(first // LANES + k):
                    lanes = slice(k * LANES + low, k * LANES + high)
                    stage_ref[at + (slice(0, modes), slice(low, high))] = state[:, lanes]
                    stage_ref[at + (slice(modes, 2 * modes), slice(low, high))] = carry[:, lanes]
                    stage_ref[at + (slice(2 * modes, 3 * modes), slice(low, high))] = local[:, lanes]
        chunks = range(i * width // LANES, (i + 1) * width // LANES)
        used = sorted({at for chunk in chunks for _, _, at in places(chunk)})
        slots, pieces = sorted({at[0] for at in used}), sorted({at[1] for at in used})
        span = (pl.ds(slots[0], len(slots)), pl.ds(pieces[0], len(pieces)))
        stores.append(pltpu.make_async_copy(stage_ref.at[span], out_ref.at[span], out_sems.at[i]))
        stores[-1].start()
    for copy in stores:
        copy.wait()


def local_grad_kernel(
    sub, rates_hbm, residues_ref, grad_hbm, out_ref, rates_ref, grad_ref, decay_ref, sems
):
    modes = rates_ref.shape[0]
    rows, channels = grad_ref.shape
    get_rates = pltpu.make_async_copy(rates_hbm, rates_ref, sems.at[0])
    get_rates.start()
    get_grad = pltpu.make_async_copy(grad_hbm.at[0], grad_ref, sems.at[1])
    get_grad.start()
    get_rates.wait()
    for r in range(modes):
        decay_ref[:, r * rows : (r + 1) * rows] = decay_matrix(rates_ref[r], rows)
    column = lax.broadcasted_iota(jnp.int32, (rows, LANES), 1) % modes
    rates = jnp.zeros((rows, LANES), jnp.float32)
    for r in range(modes):
        rates = jnp.where(column == r, rates_ref[r], rates)
    offset = lax.broadcasted_iota(jnp.int32, (rows, LANES), 0).astype(jnp.float32)
    out_ref[:, channels : channels + LANES] = mode_gain(rates) * jnp.exp(-rates * (rows - offset))
    rates = rate_column(rates_ref, modes, LANES)
    out_ref[0:modes, channels + LANES : channels + 2 * LANES] = jnp.exp(-rates * rows)
    get_grad.wait()

    @pl.loop(0, channels // sub)
    def _(i):
        part = pl.ds(pl.multiple_of(i * sub, sub), sub)
        grad32 = grad_ref[:, part].astype(jnp.float32)
        scaled = jnp.concatenate(
            [(grad32 * residues_ref[r : r + 1, part]).astype(jnp.bfloat16) for r in range(modes)],
            axis=0,
        )
        out_ref[:, part] = jnp.dot(decay_ref[...], scaled, preferred_element_type=jnp.float32)


def block_decay(local_ref, modes, width):
    last = local_ref.shape[1] - LANES
    return local_ref[0:modes, last : last + width]


def steps(count, body, start):
    return lax.fori_loop(0, count, body, start, unroll=count <= 8)


def half_kernel(batch_count, half, mask, local_ref, terms_ref, out_ref):
    modes, width = out_ref.shape[1:]
    pieces = terms_ref.shape[0] // (batch_count * half)
    decay = block_decay(local_ref, modes, width)
    zero = jnp.zeros((modes, width), jnp.float32)
    later = lax.axis_index("seq") >= half
    for k in range(pieces):

        def sequence(b, total):
            def state(j, pair):
                total, incoming = pair
                at = ((b * half + half - 1 - j) ^ mask) * pieces + k
                weights = terms_ref[at, modes : 2 * modes, :]
                total = total + (terms_ref[at, 2 * modes : 3 * modes, :] + incoming * weights)
                return total, terms_ref[at, 0:modes, :] + decay * incoming

            def weight(j, before):
                return terms_ref[((b * half + j) ^ mask) * pieces + k, modes : 2 * modes, :] + decay * before

            total, incoming = steps(half, state, (total, zero))
            out_ref[b * pieces + k] = jnp.where(later, incoming, steps(half, weight, zero))
            return total

        out_ref[batch_count * pieces + k] = steps(batch_count, sequence, zero)


def scan_kernel(batch_count, half, mask, paired, local_ref, terms_ref, own_ref, other_ref, out_ref):
    modes, width = own_ref.shape[1:]
    pieces = terms_ref.shape[0] // (batch_count * half)
    decay = block_decay(local_ref, modes, width)
    later = lax.axis_index("seq") >= half
    totals = []
    for k in range(pieces):
        last = batch_count * pieces + k
        total = own_ref[last] + other_ref[last]

        def sequence(b, total):
            other = other_ref[b * pieces + k]

            def block(j, incoming):
                at = (b * half + half - 1 - j) ^ mask
                out_ref[at, k * modes : (k + 1) * modes, :] = incoming
                return terms_ref[at * pieces + k, 0:modes, :] + decay * incoming

            steps(half, block, jnp.where(later, 0.0, other))
            return total + own_ref[b * pieces + k] * other

        totals.append(steps(batch_count, sequence, total))
    if paired:
        for at in range(batch_count * half):
            out_ref[at ^ mask, pieces * modes :, :] = totals[at // half // 2]
    else:

        def spread(at, carry):
            out_ref[at, pieces * modes :, :] = jnp.concatenate(totals, axis=0)
            return carry

        lax.fori_loop(0, batch_count * half, spread, 0, unroll=8)


def finish_kernel(slices, read_incoming, read_total, residues_ref, local_ref, back_ref, grad_hbm, sum_hbm, grad_ref, sum_ref, sems):
    modes, channels = residues_ref.shape
    rows = local_ref.shape[0]
    width = channels // slices
    carry = local_ref[:, channels : channels + 2 * modes].astype(jnp.bfloat16)
    own = sum_ref.shape[1] // LANES
    for k in range(own):
        sum_ref[:, k * LANES : (k + 1) * LANES] = read_total(back_ref, k)
    stores = [pltpu.make_async_copy(sum_ref, sum_hbm, sems.at[slices])]
    stores[0].start()
    for i in range(slices):
        pieces = []
        for chunk in range(i * width // LANES, (i + 1) * width // LANES):
            lanes = slice(chunk * LANES, (chunk + 1) * LANES)
            value = residues_ref[:, lanes] * read_incoming(back_ref, chunk)
            high = value.astype(jnp.bfloat16).astype(jnp.float32)
            pieces.append(jnp.concatenate([high, value - high], axis=0).astype(jnp.bfloat16))
        carried = jnp.dot(
            carry, jnp.concatenate(pieces, axis=1), preferred_element_type=jnp.float32
        )
        part = pl.ds(i * width, width)
        grad_ref[:, part] = (local_ref[:, part] + carried).astype(jnp.bfloat16)
        stores.append(
            pltpu.make_async_copy(grad_ref.at[:, part], grad_hbm.at[0, :, part], sems.at[i])
        )
        stores[-1].start()
    for copy in stores:
        copy.wait()


def to_owners(chunks, owners):
    count, pieces, rows, lanes = chunks.shape
    if owners == count:
        return chunks.reshape(owners, pieces * rows, lanes)
    narrow = count * lanes // owners
    parts = chunks.reshape(count, rows, lanes // narrow, narrow)
    return jnp.swapaxes(parts, 1, 2).reshape(owners, rows, narrow)


def from_owners(parts, count):
    owners, rows, narrow = parts.shape
    if owners <= count:
        return parts
    chunks = parts.reshape(count, owners // count, rows, narrow)
    return jnp.swapaxes(chunks, 1, 2).reshape(count, rows, LANES)


def params(limit=VMEM_LIMIT):
    return pltpu.CompilerParams(vmem_limit_bytes=limit)


def local(batch_count, block_count, grad_out, block_in, residues, decay_rates):
    _, rows, channels = grad_out.shape
    modes = residues.shape[0]
    half = block_count // 2
    owners = batch_count * half
    chunks = channels // LANES
    width = min(LANES, channels // owners)
    pieces = channels // (owners * width)
    anywhere = pl.BlockSpec(memory_space=pl.ANY)
    whole = pl.BlockSpec(memory_space=pltpu.VMEM)
    mask = (batch_count - 1) * half + 1 if half > 1 and owners & (owners - 1) == 0 else 0

    def exchange(slots):
        places = [d * block_count + j for d in range(batch_count) for j in range(half)]
        groups = [[first + places[p ^ mask] for p in range(owners)] for first in (0, half)]
        return lax.all_to_all(slots, ("dp", "seq"), 0, 0, axis_index_groups=groups)

    slot_count = min(owners, chunks)
    own = chunks // batch_count
    paired = slot_count == 2 * own and pieces * 2 == batch_count
    total_rows = modes if paired else pieces * modes
    if owners > chunks:
        slot = lambda owner: owner
    else:
        slot = lambda owner: owner ^ mask

    def places(chunk):
        if not paired:
            return [(0, LANES, (slot(chunk // pieces), chunk % pieces))]
        d, m = chunk // own, chunk % own
        low, high = slot(2 * m + d % 2), slot(2 * m + 1 - d % 2)
        return [(0, LANES // 2, (low, d // 2)), (LANES // 2, LANES, (high, d // 2))]

    def in_low_half():
        return lax.broadcasted_iota(jnp.int32, (modes, LANES), 1) < LANES // 2

    def read_incoming(back_ref, chunk):
        parts = [
            back_ref[at, piece * modes : (piece + 1) * modes, :] for _, _, (at, piece) in places(chunk)
        ]
        return jnp.where(in_low_half(), *parts) if paired else parts[0]

    def read_total(back_ref, m):
        d = lax.axis_index("dp")
        if paired:
            first = back_ref[slot(2 * m), pieces * modes :, :]
            second = back_ref[slot(2 * m + 1), pieces * modes :, :]
            return jnp.where(in_low_half() == (d % 2 == 0), first, second)
        chunk = d * own + m
        row = pl.multiple_of((pieces + chunk % pieces) * modes, modes)
        return back_ref[slot(chunk // pieces), pl.ds(row, modes), :]

    def reorder(slots):
        if owners <= chunks:
            return slots
        return slots[jnp.array([p ^ mask for p in range(owners)])]

    terms = pl.pallas_call(
        functools.partial(terms_kernel, 2, 256, places),
        in_specs=[anywhere] * 3,
        out_specs=anywhere,
        out_shape=jax.ShapeDtypeStruct((slot_count, pieces, 3 * modes, LANES), jnp.float32),
        scratch_shapes=[
            pltpu.SMEM((modes,), jnp.float32),
            pltpu.VMEM((rows, channels), jnp.bfloat16),
            pltpu.VMEM((rows, channels), jnp.bfloat16),
            pltpu.VMEM((modes * rows // GROUP, 2 * rows), jnp.bfloat16),
            pltpu.VMEM((modes * rows // GROUP, 2 * rows), jnp.bfloat16),
            pltpu.VMEM((GROUP, modes, LANES), jnp.float32),
            pltpu.SemaphoreType.DMA((3, 2)),
            pltpu.VMEM((slot_count, pieces, 3 * modes, LANES), jnp.float32),
            pltpu.SemaphoreType.DMA((2,)),
        ],
        compiler_params=params(FIRST_LIMIT),
        name="terms",
    )(decay_rates, grad_out, block_in)
    terms = exchange(reorder(to_owners(terms, owners)))
    terms = terms.reshape(owners * pieces, 3 * modes, width)
    local_grad = pl.pallas_call(
        functools.partial(local_grad_kernel, 512),
        in_specs=[anywhere, whole, anywhere],
        out_specs=whole,
        out_shape=jax.ShapeDtypeStruct((rows, channels + 2 * LANES), jnp.float32),
        scratch_shapes=[
            pltpu.SMEM((modes,), jnp.float32),
            pltpu.VMEM((rows, channels), jnp.bfloat16),
            pltpu.VMEM((rows, modes * rows), jnp.bfloat16),
            pltpu.SemaphoreType.DMA((2,)),
        ],
        compiler_params=params(),
        cost_estimate=pl.CostEstimate(
            flops=2 * rows * modes * rows * channels,
            bytes_accessed=6 * rows * channels,
            transcendentals=0,
        ),
        name="local_grad",
    )(decay_rates, residues, grad_out)
    cross = pl.pallas_call(
        functools.partial(half_kernel, batch_count, half, mask),
        in_specs=[whole, whole],
        out_specs=whole,
        out_shape=jax.ShapeDtypeStruct(((batch_count + 1) * pieces, modes, width), jnp.float32),
        compiler_params=params(),
        name="half",
    )(local_grad, terms)
    other = lax.ppermute(cross, "seq", [(s, (s + half) % block_count) for s in range(block_count)])
    back = pl.pallas_call(
        functools.partial(scan_kernel, batch_count, half, mask, paired),
        in_specs=[whole] * 4,
        out_specs=whole,
        out_shape=jax.ShapeDtypeStruct((owners, pieces * modes + total_rows, width), jnp.float32),
        compiler_params=params(),
        name="scan",
    )(local_grad, terms, cross, other)
    back = from_owners(reorder(exchange(back)), chunks)
    return pl.pallas_call(
        functools.partial(finish_kernel, 4, read_incoming, read_total),
        in_specs=[whole] * 3,
        out_specs=[anywhere, anywhere],
        out_shape=[
            jax.ShapeDtypeStruct((1, rows, channels), jnp.bfloat16),
            jax.ShapeDtypeStruct((modes, channels // batch_count), jnp.float32),
        ],
        scratch_shapes=[
            pltpu.VMEM((rows, channels), jnp.bfloat16),
            pltpu.VMEM((modes, channels // batch_count), jnp.float32),
            pltpu.SemaphoreType.DMA((5,)),
        ],
        compiler_params=params(),
        name="finish",
    )(residues, local_grad, back)


def solution(mesh):
    placed = (P("dp", "seq", None), P("dp", "seq", None), P(), P())
    return jax.shard_map(
        functools.partial(local, mesh.shape["dp"], mesh.shape["seq"]),
        mesh=mesh,
        in_specs=placed,
        out_specs=(P("dp", "seq", None), P(None, "dp")),
        check_vma=False,
    )
```

```python
import functools

import jax
import jax.numpy as jnp
from jax import lax
from jax.experimental import pallas as pl
from jax.experimental.pallas import tpu as pltpu
from jax.sharding import PartitionSpec as P

VMEM_LIMIT = 48 * 1024 * 1024
FIRST_LIMIT = 60 * 1024 * 1024
LANES = 128
SUBLANES = 8
GROUP = 4


def rate_column(rates_ref, mode_count, width):
    rows = lax.broadcasted_iota(jnp.int32, (mode_count, width), 0)
    column = jnp.zeros((mode_count, width), jnp.float32)
    for r in range(mode_count):
        column = jnp.where(rows == r, rates_ref[r], column)
    return column


def mode_gain(rates):
    return jnp.sqrt(1.0 - jnp.exp(-2.0 * rates))


def decay_matrix(rate, rows):
    earlier = lax.broadcasted_iota(jnp.int32, (rows, rows), 0)
    later = lax.broadcasted_iota(jnp.int32, (rows, rows), 1)
    lag = (later - earlier).astype(jnp.float32)
    rates = jnp.full((rows, rows), rate, jnp.float32)
    gain = mode_gain(jnp.full((SUBLANES, rows), rate, jnp.float32))[:1]
    table = gain * jnp.exp(-rates * jnp.maximum(lag, 0.0))
    return jnp.where(lag >= 0.0, table, 0.0).astype(jnp.bfloat16)


def split_bf16(value):
    high = value.astype(jnp.bfloat16)
    return high, (value - high.astype(jnp.float32)).astype(jnp.bfloat16)


def terms_kernel(
    slices,
    sub,
    places,
    rates_hbm,
    grad_hbm,
    in_hbm,
    out_ref,
    rates_ref,
    grad_ref,
    in_ref,
    before_ref,
    after_ref,
    lag_ref,
    sems,
    stage_ref,
    out_sems,
):
    modes = rates_ref.shape[0]
    rows, channels = grad_ref.shape
    width = channels // slices
    groups = rows // GROUP
    get_rates = pltpu.make_async_copy(rates_hbm, rates_ref, sems.at[2, 0])
    get_rates.start()
    loads = []
    for i in range(slices):
        part = pl.ds(i * width, width)
        pair = (
            pltpu.make_async_copy(grad_hbm.at[0, :, part], grad_ref.at[:, part], sems.at[0, i]),
            pltpu.make_async_copy(in_hbm.at[0, :, part], in_ref.at[:, part], sems.at[1, i]),
        )
        for copy in pair:
            copy.start()
        loads.append(pair)
    get_rates.wait()
    rates = rate_column(rates_ref, modes, rows)
    gain = mode_gain(rates)
    position = lax.broadcasted_iota(jnp.int32, (modes, rows), 1)
    offset = position.astype(jnp.float32)
    for u in range(1, groups + 1):
        at = slice((u - 1) * modes, u * modes)
        edge = u * GROUP
        before = gain * jnp.exp(-rates * jnp.maximum(edge - offset, 0.0))
        if u < groups:
            after = jnp.exp(-rates * jnp.maximum(offset - edge, 0.0))
            after = jnp.where((position >= edge) & (position < edge + GROUP), after, 0.0)
            high, low = split_bf16(jnp.where(position < edge, before, 0.0))
            after_high, after_low = split_bf16(after)
        else:
            high, low = before.astype(jnp.bfloat16), jnp.zeros((modes, rows), jnp.bfloat16)
            after_high, after_low = jnp.exp(-rates * offset).astype(jnp.bfloat16), low
        before_ref[at, 0:rows] = high
        before_ref[at, rows : 2 * rows] = low
        after_ref[at, 0:rows] = after_high
        after_ref[at, rows : 2 * rows] = after_low
    for k in range(GROUP):
        lag_ref[k] = (gain * jnp.exp(-rates * k))[:, :LANES]

    in_group = lax.broadcasted_iota(jnp.int32, (SUBLANES, sub), 0) % GROUP
    stores = []
    for i in range(slices):
        for copy in loads[i]:
            copy.wait()
        for first in range(i * width, (i + 1) * width, sub):
            part = slice(first, first + sub)
            grad = grad_ref[:, part]
            block = in_ref[:, part]
            twice = jnp.concatenate([block, block], axis=0)
            sums = jnp.dot(before_ref[...], twice, preferred_element_type=jnp.float32)
            twice = jnp.concatenate([grad, grad], axis=0)
            states = jnp.dot(after_ref[...], twice, preferred_element_type=jnp.float32)
            last = slice((groups - 1) * modes, groups * modes)
            carry, state = sums[last], states[last]
            local = sums[0:modes] * states[0:modes]
            for u in range(1, groups - 1):
                at = slice(u * modes, (u + 1) * modes)
                local = local + sums[at] * states[at]
            grad32 = grad.astype(jnp.float32).reshape(rows // SUBLANES, SUBLANES, sub)
            block32 = block.astype(jnp.float32).reshape(rows // SUBLANES, SUBLANES, sub)
            for k in range(GROUP):
                later = pltpu.roll(grad32, SUBLANES - k, 1) if k else grad32
                product = jnp.sum(block32 * later, axis=0)
                if k:
                    product = jnp.where(in_group + k < GROUP, product, 0.0)
                weight = jnp.concatenate([lag_ref[k]] * (sub // LANES), axis=1)
                local = local + weight * jnp.sum(product, axis=0, keepdims=True)
            for k in range(sub // LANES):
                for low, high, at in places(first // LANES + k):
                    lanes = slice(k * LANES + low, k * LANES + high)
                    stage_ref[at + (slice(0, modes), slice(low, high))] = state[:, lanes]
                    stage_ref[at + (slice(modes, 2 * modes), slice(low, high))] = carry[:, lanes]
                    stage_ref[at + (slice(2 * modes, 3 * modes), slice(low, high))] = local[:, lanes]
        chunks = range(i * width // LANES, (i + 1) * width // LANES)
        used = sorted({at for chunk in chunks for _, _, at in places(chunk)})
        slots, pieces = sorted({at[0] for at in used}), sorted({at[1] for at in used})
        span = (pl.ds(slots[0], len(slots)), pl.ds(pieces[0], len(pieces)))
        stores.append(pltpu.make_async_copy(stage_ref.at[span], out_ref.at[span], out_sems.at[i]))
        stores[-1].start()
    for copy in stores:
        copy.wait()


def local_grad_kernel(
    sub, rates_hbm, residues_ref, grad_hbm, out_ref, rates_ref, grad_ref, decay_ref, sems
):
    modes = rates_ref.shape[0]
    rows, channels = grad_ref.shape
    get_rates = pltpu.make_async_copy(rates_hbm, rates_ref, sems.at[0])
    get_rates.start()
    get_grad = pltpu.make_async_copy(grad_hbm.at[0], grad_ref, sems.at[1])
    get_grad.start()
    get_rates.wait()
    for r in range(modes):
        decay_ref[:, r * rows : (r + 1) * rows] = decay_matrix(rates_ref[r], rows)
    column = lax.broadcasted_iota(jnp.int32, (rows, LANES), 1) % modes
    rates = jnp.zeros((rows, LANES), jnp.float32)
    for r in range(modes):
        rates = jnp.where(column == r, rates_ref[r], rates)
    offset = lax.broadcasted_iota(jnp.int32, (rows, LANES), 0).astype(jnp.float32)
    out_ref[:, channels : channels + LANES] = mode_gain(rates) * jnp.exp(-rates * (rows - offset))
    rates = rate_column(rates_ref, modes, LANES)
    out_ref[0:modes, channels + LANES : channels + 2 * LANES] = jnp.exp(-rates * rows)
    get_grad.wait()

    @pl.loop(0, channels // sub)
    def _(i):
        part = pl.ds(pl.multiple_of(i * sub, sub), sub)
        grad32 = grad_ref[:, part].astype(jnp.float32)
        scaled = jnp.concatenate(
            [(grad32 * residues_ref[r : r + 1, part]).astype(jnp.bfloat16) for r in range(modes)],
            axis=0,
        )
        out_ref[:, part] = jnp.dot(decay_ref[...], scaled, preferred_element_type=jnp.float32)


def block_decay(local_ref, modes, width):
    last = local_ref.shape[1] - LANES
    return local_ref[0:modes, last : last + width]


def place(b, j, half):
    return (b // 2 * half + j) * 2 + b % 2


def steps(count, body, start):
    return lax.fori_loop(0, count, body, start, unroll=count <= 8)


def half_kernel(batch_count, half, mask, local_ref, terms_ref, out_ref):
    modes, width = out_ref.shape[1:]
    pieces = terms_ref.shape[0] // (batch_count * half)
    decay = block_decay(local_ref, modes, width)
    zero = jnp.zeros((modes, width), jnp.float32)
    later = lax.axis_index("seq") >= half
    for k in range(pieces):

        def sequence(b, total):
            def state(j, pair):
                total, incoming = pair
                at = (place(b, half - 1 - j, half) ^ mask) * pieces + k
                weights = terms_ref[at, modes : 2 * modes, :]
                total = total + (terms_ref[at, 2 * modes : 3 * modes, :] + incoming * weights)
                return total, terms_ref[at, 0:modes, :] + decay * incoming

            def weight(j, before):
                return terms_ref[(place(b, j, half) ^ mask) * pieces + k, modes : 2 * modes, :] + decay * before

            total, incoming = steps(half, state, (total, zero))
            out_ref[b * pieces + k] = jnp.where(later, incoming, steps(half, weight, zero))
            return total

        out_ref[batch_count * pieces + k] = steps(batch_count, sequence, zero)


def scan_kernel(batch_count, half, mask, paired, local_ref, terms_ref, own_ref, other_ref, out_ref):
    modes, width = own_ref.shape[1:]
    pieces = terms_ref.shape[0] // (batch_count * half)
    decay = block_decay(local_ref, modes, width)
    later = lax.axis_index("seq") >= half
    totals = []
    for k in range(pieces):
        last = batch_count * pieces + k
        total = own_ref[last] + other_ref[last]

        def sequence(b, total):
            other = other_ref[b * pieces + k]

            def block(j, incoming):
                at = place(b, half - 1 - j, half) ^ mask
                out_ref[at, k * modes : (k + 1) * modes, :] = incoming
                return terms_ref[at * pieces + k, 0:modes, :] + decay * incoming

            steps(half, block, jnp.where(later, 0.0, other))
            return total + own_ref[b * pieces + k] * other

        totals.append(steps(batch_count, sequence, total))
    if paired:
        for b in range(batch_count):
            for j in range(half):
                out_ref[place(b, j, half) ^ mask, pieces * modes :, :] = totals[b // 2]
    else:

        def spread(at, carry):
            out_ref[at, pieces * modes :, :] = jnp.concatenate(totals, axis=0)
            return carry

        lax.fori_loop(0, batch_count * half, spread, 0, unroll=8)


def finish_kernel(slices, read_incoming, read_total, residues_ref, local_ref, back_ref, grad_hbm, sum_hbm, grad_ref, sum_ref, sems):
    modes, channels = residues_ref.shape
    rows = local_ref.shape[0]
    width = channels // slices
    carry = local_ref[:, channels : channels + 2 * modes].astype(jnp.bfloat16)
    own = sum_ref.shape[1] // LANES
    for k in range(own):
        sum_ref[:, k * LANES : (k + 1) * LANES] = read_total(back_ref, k)
    stores = [pltpu.make_async_copy(sum_ref, sum_hbm, sems.at[slices])]
    stores[0].start()
    for i in range(slices):
        pieces = []
        for chunk in range(i * width // LANES, (i + 1) * width // LANES):
            lanes = slice(chunk * LANES, (chunk + 1) * LANES)
            value = residues_ref[:, lanes] * read_incoming(back_ref, chunk)
            high = value.astype(jnp.bfloat16).astype(jnp.float32)
            pieces.append(jnp.concatenate([high, value - high], axis=0).astype(jnp.bfloat16))
        carried = jnp.dot(
            carry, jnp.concatenate(pieces, axis=1), preferred_element_type=jnp.float32
        )
        part = pl.ds(i * width, width)
        grad_ref[:, part] = (local_ref[:, part] + carried).astype(jnp.bfloat16)
        stores.append(
            pltpu.make_async_copy(grad_ref.at[:, part], grad_hbm.at[0, :, part], sems.at[i])
        )
        stores[-1].start()
    for copy in stores:
        copy.wait()


def to_owners(chunks, owners):
    count, pieces, rows, lanes = chunks.shape
    if owners == count:
        return chunks.reshape(owners, pieces * rows, lanes)
    narrow = count * lanes // owners
    parts = chunks.reshape(count, rows, lanes // narrow, narrow)
    return jnp.swapaxes(parts, 1, 2).reshape(owners, rows, narrow)


def from_owners(parts, count):
    owners, rows, narrow = parts.shape
    if owners <= count:
        return parts
    chunks = parts.reshape(count, owners // count, rows, narrow)
    return jnp.swapaxes(chunks, 1, 2).reshape(count, rows, LANES)


def params(limit=VMEM_LIMIT):
    return pltpu.CompilerParams(vmem_limit_bytes=limit)


def local(batch_count, block_count, grad_out, block_in, residues, decay_rates):
    _, rows, channels = grad_out.shape
    modes = residues.shape[0]
    half = block_count // 2
    owners = batch_count * half
    chunks = channels // LANES
    width = min(LANES, channels // owners)
    pieces = channels // (owners * width)
    anywhere = pl.BlockSpec(memory_space=pl.ANY)
    whole = pl.BlockSpec(memory_space=pltpu.VMEM)
    mask = place(batch_count - 1, 1, half) if half > 1 and owners & (owners - 1) == 0 else 0

    def exchange(slots):
        where = {
            place(d, j, half) ^ mask: d * block_count + j for d in range(batch_count) for j in range(half)
        }
        groups = [[first + where[p] for p in range(owners)] for first in (0, half)]
        return lax.all_to_all(slots, ("dp", "seq"), 0, 0, axis_index_groups=groups)

    slot_count = min(owners, chunks)
    own = chunks // batch_count
    paired = slot_count == 2 * own and pieces * 2 == batch_count
    total_rows = modes if paired else pieces * modes
    if owners > chunks:
        slot = lambda owner: owner
    else:
        slot = lambda owner: owner ^ mask

    def places(chunk):
        if not paired:
            return [(0, LANES, (slot(chunk // pieces), chunk % pieces))]
        d, m = chunk // own, chunk % own
        low, high = slot(2 * m + d % 2), slot(2 * m + 1 - d % 2)
        return [(0, LANES // 2, (low, d // 2)), (LANES // 2, LANES, (high, d // 2))]

    def in_low_half():
        return lax.broadcasted_iota(jnp.int32, (modes, LANES), 1) < LANES // 2

    def read_incoming(back_ref, chunk):
        parts = [
            back_ref[at, piece * modes : (piece + 1) * modes, :] for _, _, (at, piece) in places(chunk)
        ]
        return jnp.where(in_low_half(), *parts) if paired else parts[0]

    def read_total(back_ref, m):
        d = lax.axis_index("dp")
        if paired:
            first = back_ref[slot(2 * m), pieces * modes :, :]
            second = back_ref[slot(2 * m + 1), pieces * modes :, :]
            return jnp.where(in_low_half() == (d % 2 == 0), first, second)
        chunk = d * own + m
        row = pl.multiple_of((pieces + chunk % pieces) * modes, modes)
        return back_ref[slot(chunk // pieces), pl.ds(row, modes), :]

    def reorder(slots):
        if owners <= chunks:
            return slots
        return slots[jnp.array([p ^ mask for p in range(owners)])]

    terms = pl.pallas_call(
        functools.partial(terms_kernel, 2, 256, places),
        in_specs=[anywhere] * 3,
        out_specs=anywhere,
        out_shape=jax.ShapeDtypeStruct((slot_count, pieces, 3 * modes, LANES), jnp.float32),
        scratch_shapes=[
            pltpu.SMEM((modes,), jnp.float32),
            pltpu.VMEM((rows, channels), jnp.bfloat16),
            pltpu.VMEM((rows, channels), jnp.bfloat16),
            pltpu.VMEM((modes * rows // GROUP, 2 * rows), jnp.bfloat16),
            pltpu.VMEM((modes * rows // GROUP, 2 * rows), jnp.bfloat16),
            pltpu.VMEM((GROUP, modes, LANES), jnp.float32),
            pltpu.SemaphoreType.DMA((3, 2)),
            pltpu.VMEM((slot_count, pieces, 3 * modes, LANES), jnp.float32),
            pltpu.SemaphoreType.DMA((2,)),
        ],
        compiler_params=params(FIRST_LIMIT),
        name="terms",
    )(decay_rates, grad_out, block_in)
    terms = exchange(reorder(to_owners(terms, owners)))
    terms = terms.reshape(owners * pieces, 3 * modes, width)
    local_grad = pl.pallas_call(
        functools.partial(local_grad_kernel, 512),
        in_specs=[anywhere, whole, anywhere],
        out_specs=whole,
        out_shape=jax.ShapeDtypeStruct((rows, channels + 2 * LANES), jnp.float32),
        scratch_shapes=[
            pltpu.SMEM((modes,), jnp.float32),
            pltpu.VMEM((rows, channels), jnp.bfloat16),
            pltpu.VMEM((rows, modes * rows), jnp.bfloat16),
            pltpu.SemaphoreType.DMA((2,)),
        ],
        compiler_params=params(),
        cost_estimate=pl.CostEstimate(
            flops=2 * rows * modes * rows * channels,
            bytes_accessed=6 * rows * channels,
            transcendentals=0,
        ),
        name="local_grad",
    )(decay_rates, residues, grad_out)
    cross = pl.pallas_call(
        functools.partial(half_kernel, batch_count, half, mask),
        in_specs=[whole, whole],
        out_specs=whole,
        out_shape=jax.ShapeDtypeStruct(((batch_count + 1) * pieces, modes, width), jnp.float32),
        compiler_params=params(),
        name="half",
    )(local_grad, terms)
    other = lax.ppermute(cross, "seq", [(s, (s + half) % block_count) for s in range(block_count)])
    back = pl.pallas_call(
        functools.partial(scan_kernel, batch_count, half, mask, paired),
        in_specs=[whole] * 4,
        out_specs=whole,
        out_shape=jax.ShapeDtypeStruct((owners, pieces * modes + total_rows, width), jnp.float32),
        compiler_params=params(),
        name="scan",
    )(local_grad, terms, cross, other)
    back = from_owners(reorder(exchange(back)), chunks)
    return pl.pallas_call(
        functools.partial(finish_kernel, 4, read_incoming, read_total),
        in_specs=[whole] * 3,
        out_specs=[anywhere, anywhere],
        out_shape=[
            jax.ShapeDtypeStruct((1, rows, channels), jnp.bfloat16),
            jax.ShapeDtypeStruct((modes, channels // batch_count), jnp.float32),
        ],
        scratch_shapes=[
            pltpu.VMEM((rows, channels), jnp.bfloat16),
            pltpu.VMEM((modes, channels // batch_count), jnp.float32),
            pltpu.SemaphoreType.DMA((5,)),
        ],
        compiler_params=params(),
        name="finish",
    )(residues, local_grad, back)


def solution(mesh):
    placed = (P("dp", "seq", None), P("dp", "seq", None), P(), P())
    return jax.shard_map(
        functools.partial(local, mesh.shape["dp"], mesh.shape["seq"]),
        mesh=mesh,
        in_specs=placed,
        out_specs=(P("dp", "seq", None), P(None, "dp")),
        check_vma=False,
    )
```

```python
import functools

import jax
import jax.numpy as jnp
from jax import lax
from jax.experimental import pallas as pl
from jax.experimental.pallas import tpu as pltpu
from jax.sharding import PartitionSpec as P

VMEM_LIMIT = 48 * 1024 * 1024
FIRST_LIMIT = 60 * 1024 * 1024
LANES = 128
SUBLANES = 8
GROUP = 4


def rate_column(rates_ref, mode_count, width):
    rows = lax.broadcasted_iota(jnp.int32, (mode_count, width), 0)
    column = jnp.zeros((mode_count, width), jnp.float32)
    for r in range(mode_count):
        column = jnp.where(rows == r, rates_ref[r], column)
    return column


def mode_gain(rates):
    return jnp.sqrt(1.0 - jnp.exp(-2.0 * rates))


def decay_matrix(rate, rows):
    earlier = lax.broadcasted_iota(jnp.int32, (rows, rows), 0)
    later = lax.broadcasted_iota(jnp.int32, (rows, rows), 1)
    lag = (later - earlier).astype(jnp.float32)
    rates = jnp.full((rows, rows), rate, jnp.float32)
    gain = mode_gain(jnp.full((SUBLANES, rows), rate, jnp.float32))[:1]
    table = gain * jnp.exp(-rates * jnp.maximum(lag, 0.0))
    return jnp.where(lag >= 0.0, table, 0.0).astype(jnp.bfloat16)


def split_bf16(value):
    high = value.astype(jnp.bfloat16)
    return high, (value - high.astype(jnp.float32)).astype(jnp.bfloat16)


def terms_kernel(
    slices,
    sub,
    places,
    rates_hbm,
    grad_hbm,
    in_hbm,
    out_ref,
    rates_ref,
    grad_ref,
    in_ref,
    before_ref,
    after_ref,
    lag_ref,
    sems,
    stage_ref,
    out_sems,
):
    modes = rates_ref.shape[0]
    rows, channels = grad_ref.shape
    width = channels // slices
    groups = rows // GROUP
    get_rates = pltpu.make_async_copy(rates_hbm, rates_ref, sems.at[2, 0])
    get_rates.start()
    loads = []
    for i in range(slices):
        part = pl.ds(i * width, width)
        pair = (
            pltpu.make_async_copy(grad_hbm.at[0, :, part], grad_ref.at[:, part], sems.at[0, i]),
            pltpu.make_async_copy(in_hbm.at[0, :, part], in_ref.at[:, part], sems.at[1, i]),
        )
        for copy in pair:
            copy.start()
        loads.append(pair)
    get_rates.wait()
    rates = rate_column(rates_ref, modes, rows)
    gain = mode_gain(rates)
    position = lax.broadcasted_iota(jnp.int32, (modes, rows), 1)
    offset = position.astype(jnp.float32)
    for u in range(1, groups + 1):
        at = slice((u - 1) * modes, u * modes)
        edge = u * GROUP
        before = gain * jnp.exp(-rates * jnp.maximum(edge - offset, 0.0))
        if u < groups:
            after = jnp.exp(-rates * jnp.maximum(offset - edge, 0.0))
            after = jnp.where((position >= edge) & (position < edge + GROUP), after, 0.0)
            high, low = split_bf16(jnp.where(position < edge, before, 0.0))
            after_high, after_low = split_bf16(after)
        else:
            high, low = before.astype(jnp.bfloat16), jnp.zeros((modes, rows), jnp.bfloat16)
            after_high, after_low = jnp.exp(-rates * offset).astype(jnp.bfloat16), low
        before_ref[at, 0:rows] = high
        before_ref[at, rows : 2 * rows] = low
        after_ref[at, 0:rows] = after_high
        after_ref[at, rows : 2 * rows] = after_low
    for k in range(GROUP):
        lag_ref[k] = (gain * jnp.exp(-rates * k))[:, :LANES]

    in_group = lax.broadcasted_iota(jnp.int32, (SUBLANES, sub), 0) % GROUP
    stores = []
    for i in range(slices):
        for copy in loads[i]:
            copy.wait()
        for first in range(i * width, (i + 1) * width, sub):
            part = slice(first, first + sub)
            grad = grad_ref[:, part]
            block = in_ref[:, part]
            near = jnp.zeros((modes, sub), jnp.float32)
            grad32 = grad.astype(jnp.float32).reshape(rows // SUBLANES, SUBLANES, sub)
            block32 = block.astype(jnp.float32).reshape(rows // SUBLANES, SUBLANES, sub)
            for k in range(GROUP):
                later = pltpu.roll(grad32, SUBLANES - k, 1) if k else grad32
                product = jnp.sum(block32 * later, axis=0)
                if k:
                    product = jnp.where(in_group + k < GROUP, product, 0.0)
                weight = jnp.concatenate([lag_ref[k]] * (sub // LANES), axis=1)
                near = near + weight * jnp.sum(product, axis=0, keepdims=True)
            twice = jnp.concatenate([block, block], axis=0)
            sums = jnp.dot(before_ref[...], twice, preferred_element_type=jnp.float32)
            twice = jnp.concatenate([grad, grad], axis=0)
            states = jnp.dot(after_ref[...], twice, preferred_element_type=jnp.float32)
            last = slice((groups - 1) * modes, groups * modes)
            carry, state = sums[last], states[last]
            lines = [None] * 4
            for u in range(groups - 1):
                at = slice(u * modes, (u + 1) * modes)
                product = sums[at] * states[at]
                lines[u % 4] = product if u < 4 else lines[u % 4] + product
            local = sum(lines, near)
            for k in range(sub // LANES):
                for low, high, at in places(first // LANES + k):
                    lanes = slice(k * LANES + low, k * LANES + high)
                    stage_ref[at + (slice(0, modes), slice(low, high))] = state[:, lanes]
                    stage_ref[at + (slice(modes, 2 * modes), slice(low, high))] = carry[:, lanes]
                    stage_ref[at + (slice(2 * modes, 3 * modes), slice(low, high))] = local[:, lanes]
        chunks = range(i * width // LANES, (i + 1) * width // LANES)
        used = sorted({at for chunk in chunks for _, _, at in places(chunk)})
        slots, pieces = sorted({at[0] for at in used}), sorted({at[1] for at in used})
        span = (pl.ds(slots[0], len(slots)), pl.ds(pieces[0], len(pieces)))
        stores.append(pltpu.make_async_copy(stage_ref.at[span], out_ref.at[span], out_sems.at[i]))
        stores[-1].start()
    for copy in stores:
        copy.wait()


def local_grad_kernel(
    sub, rates_hbm, residues_ref, grad_hbm, out_ref, rates_ref, grad_ref, decay_ref, sems
):
    modes = rates_ref.shape[0]
    rows, channels = grad_ref.shape
    get_rates = pltpu.make_async_copy(rates_hbm, rates_ref, sems.at[0])
    get_rates.start()
    get_grad = pltpu.make_async_copy(grad_hbm.at[0], grad_ref, sems.at[1])
    get_grad.start()
    get_rates.wait()
    for r in range(modes):
        decay_ref[:, r * rows : (r + 1) * rows] = decay_matrix(rates_ref[r], rows)
    column = lax.broadcasted_iota(jnp.int32, (rows, LANES), 1) % modes
    rates = jnp.zeros((rows, LANES), jnp.float32)
    for r in range(modes):
        rates = jnp.where(column == r, rates_ref[r], rates)
    offset = lax.broadcasted_iota(jnp.int32, (rows, LANES), 0).astype(jnp.float32)
    out_ref[:, channels : channels + LANES] = mode_gain(rates) * jnp.exp(-rates * (rows - offset))
    rates = rate_column(rates_ref, modes, LANES)
    out_ref[0:modes, channels + LANES : channels + 2 * LANES] = jnp.exp(-rates * rows)
    get_grad.wait()

    @pl.loop(0, channels // sub)
    def _(i):
        part = pl.ds(pl.multiple_of(i * sub, sub), sub)
        grad32 = grad_ref[:, part].astype(jnp.float32)
        scaled = jnp.concatenate(
            [(grad32 * residues_ref[r : r + 1, part]).astype(jnp.bfloat16) for r in range(modes)],
            axis=0,
        )
        out_ref[:, part] = jnp.dot(decay_ref[...], scaled, preferred_element_type=jnp.float32)


def block_decay(local_ref, modes, width):
    last = local_ref.shape[1] - LANES
    return local_ref[0:modes, last : last + width]


def place(b, j, half):
    return (b // 2 * half + j) * 2 + b % 2


def steps(count, body, start):
    return lax.fori_loop(0, count, body, start, unroll=count <= 8)


def half_kernel(batch_count, half, mask, local_ref, terms_ref, out_ref):
    modes, width = out_ref.shape[1:]
    pieces = terms_ref.shape[0] // (batch_count * half)
    decay = block_decay(local_ref, modes, width)
    zero = jnp.zeros((modes, width), jnp.float32)
    later = lax.axis_index("seq") >= half
    for k in range(pieces):

        def sequence(b, total):
            def state(j, pair):
                total, incoming = pair
                at = (place(b, half - 1 - j, half) ^ mask) * pieces + k
                weights = terms_ref[at, modes : 2 * modes, :]
                total = total + (terms_ref[at, 2 * modes : 3 * modes, :] + incoming * weights)
                return total, terms_ref[at, 0:modes, :] + decay * incoming

            def weight(j, before):
                return terms_ref[(place(b, j, half) ^ mask) * pieces + k, modes : 2 * modes, :] + decay * before

            total, incoming = steps(half, state, (total, zero))
            out_ref[b * pieces + k] = jnp.where(later, incoming, steps(half, weight, zero))
            return total

        out_ref[batch_count * pieces + k] = steps(batch_count, sequence, zero)


def scan_kernel(batch_count, half, mask, paired, local_ref, terms_ref, own_ref, other_ref, out_ref):
    modes, width = own_ref.shape[1:]
    pieces = terms_ref.shape[0] // (batch_count * half)
    decay = block_decay(local_ref, modes, width)
    later = lax.axis_index("seq") >= half
    totals = []
    for k in range(pieces):
        last = batch_count * pieces + k
        total = own_ref[last] + other_ref[last]

        def sequence(b, total):
            other = other_ref[b * pieces + k]

            def block(j, incoming):
                at = place(b, half - 1 - j, half) ^ mask
                out_ref[at, k * modes : (k + 1) * modes, :] = incoming
                return terms_ref[at * pieces + k, 0:modes, :] + decay * incoming

            steps(half, block, jnp.where(later, 0.0, other))
            return total + own_ref[b * pieces + k] * other

        totals.append(steps(batch_count, sequence, total))
    if paired:
        for b in range(batch_count):
            for j in range(half):
                out_ref[place(b, j, half) ^ mask, pieces * modes :, :] = totals[b // 2]
    else:

        def spread(at, carry):
            out_ref[at, pieces * modes :, :] = jnp.concatenate(totals, axis=0)
            return carry

        lax.fori_loop(0, batch_count * half, spread, 0, unroll=8)


def finish_kernel(slices, read_incoming, read_total, residues_ref, local_ref, back_ref, grad_hbm, sum_hbm, grad_ref, sum_ref, sems):
    modes, channels = residues_ref.shape
    rows = local_ref.shape[0]
    width = channels // slices
    carry = local_ref[:, channels : channels + 2 * modes].astype(jnp.bfloat16)
    own = sum_ref.shape[1] // LANES
    for k in range(own):
        sum_ref[:, k * LANES : (k + 1) * LANES] = read_total(back_ref, k)
    stores = [pltpu.make_async_copy(sum_ref, sum_hbm, sems.at[slices])]
    stores[0].start()
    for i in range(slices):
        pieces = []
        for chunk in range(i * width // LANES, (i + 1) * width // LANES):
            lanes = slice(chunk * LANES, (chunk + 1) * LANES)
            value = residues_ref[:, lanes] * read_incoming(back_ref, chunk)
            high = value.astype(jnp.bfloat16).astype(jnp.float32)
            pieces.append(jnp.concatenate([high, value - high], axis=0).astype(jnp.bfloat16))
        carried = jnp.dot(
            carry, jnp.concatenate(pieces, axis=1), preferred_element_type=jnp.float32
        )
        part = pl.ds(i * width, width)
        grad_ref[:, part] = (local_ref[:, part] + carried).astype(jnp.bfloat16)
        stores.append(
            pltpu.make_async_copy(grad_ref.at[:, part], grad_hbm.at[0, :, part], sems.at[i])
        )
        stores[-1].start()
    for copy in stores:
        copy.wait()


def to_owners(chunks, owners):
    count, pieces, rows, lanes = chunks.shape
    if owners == count:
        return chunks.reshape(owners, pieces * rows, lanes)
    narrow = count * lanes // owners
    parts = chunks.reshape(count, rows, lanes // narrow, narrow)
    return jnp.swapaxes(parts, 1, 2).reshape(owners, rows, narrow)


def from_owners(parts, count):
    owners, rows, narrow = parts.shape
    if owners <= count:
        return parts
    chunks = parts.reshape(count, owners // count, rows, narrow)
    return jnp.swapaxes(chunks, 1, 2).reshape(count, rows, LANES)


def params(limit=VMEM_LIMIT):
    return pltpu.CompilerParams(vmem_limit_bytes=limit)


def local(batch_count, block_count, grad_out, block_in, residues, decay_rates):
    _, rows, channels = grad_out.shape
    modes = residues.shape[0]
    half = block_count // 2
    owners = batch_count * half
    chunks = channels // LANES
    width = min(LANES, channels // owners)
    pieces = channels // (owners * width)
    anywhere = pl.BlockSpec(memory_space=pl.ANY)
    whole = pl.BlockSpec(memory_space=pltpu.VMEM)
    mask = place(batch_count - 1, 1, half) if half > 1 and owners & (owners - 1) == 0 else 0

    def exchange(slots):
        where = {
            place(d, j, half) ^ mask: d * block_count + j for d in range(batch_count) for j in range(half)
        }
        groups = [[first + where[p] for p in range(owners)] for first in (0, half)]
        return lax.all_to_all(slots, ("dp", "seq"), 0, 0, axis_index_groups=groups)

    slot_count = min(owners, chunks)
    own = chunks // batch_count
    paired = slot_count == 2 * own and pieces * 2 == batch_count
    total_rows = modes if paired else pieces * modes
    if owners > chunks:
        slot = lambda owner: owner
    else:
        slot = lambda owner: owner ^ mask

    def places(chunk):
        if not paired:
            return [(0, LANES, (slot(chunk // pieces), chunk % pieces))]
        d, m = chunk // own, chunk % own
        low, high = slot(2 * m + d % 2), slot(2 * m + 1 - d % 2)
        return [(0, LANES // 2, (low, d // 2)), (LANES // 2, LANES, (high, d // 2))]

    def in_low_half():
        return lax.broadcasted_iota(jnp.int32, (modes, LANES), 1) < LANES // 2

    def read_incoming(back_ref, chunk):
        parts = [
            back_ref[at, piece * modes : (piece + 1) * modes, :] for _, _, (at, piece) in places(chunk)
        ]
        return jnp.where(in_low_half(), *parts) if paired else parts[0]

    def read_total(back_ref, m):
        d = lax.axis_index("dp")
        if paired:
            first = back_ref[slot(2 * m), pieces * modes :, :]
            second = back_ref[slot(2 * m + 1), pieces * modes :, :]
            return jnp.where(in_low_half() == (d % 2 == 0), first, second)
        chunk = d * own + m
        row = pl.multiple_of((pieces + chunk % pieces) * modes, modes)
        return back_ref[slot(chunk // pieces), pl.ds(row, modes), :]

    def reorder(slots):
        if owners <= chunks:
            return slots
        return slots[jnp.array([p ^ mask for p in range(owners)])]

    terms = pl.pallas_call(
        functools.partial(terms_kernel, 2, 256, places),
        in_specs=[anywhere] * 3,
        out_specs=anywhere,
        out_shape=jax.ShapeDtypeStruct((slot_count, pieces, 3 * modes, LANES), jnp.float32),
        scratch_shapes=[
            pltpu.SMEM((modes,), jnp.float32),
            pltpu.VMEM((rows, channels), jnp.bfloat16),
            pltpu.VMEM((rows, channels), jnp.bfloat16),
            pltpu.VMEM((modes * rows // GROUP, 2 * rows), jnp.bfloat16),
            pltpu.VMEM((modes * rows // GROUP, 2 * rows), jnp.bfloat16),
            pltpu.VMEM((GROUP, modes, LANES), jnp.float32),
            pltpu.SemaphoreType.DMA((3, 2)),
            pltpu.VMEM((slot_count, pieces, 3 * modes, LANES), jnp.float32),
            pltpu.SemaphoreType.DMA((2,)),
        ],
        compiler_params=params(FIRST_LIMIT),
        name="terms",
    )(decay_rates, grad_out, block_in)
    terms = exchange(reorder(to_owners(terms, owners)))
    terms = terms.reshape(owners * pieces, 3 * modes, width)
    local_grad = pl.pallas_call(
        functools.partial(local_grad_kernel, 512),
        in_specs=[anywhere, whole, anywhere],
        out_specs=whole,
        out_shape=jax.ShapeDtypeStruct((rows, channels + 2 * LANES), jnp.float32),
        scratch_shapes=[
            pltpu.SMEM((modes,), jnp.float32),
            pltpu.VMEM((rows, channels), jnp.bfloat16),
            pltpu.VMEM((rows, modes * rows), jnp.bfloat16),
            pltpu.SemaphoreType.DMA((2,)),
        ],
        compiler_params=params(),
        cost_estimate=pl.CostEstimate(
            flops=2 * rows * modes * rows * channels,
            bytes_accessed=6 * rows * channels,
            transcendentals=0,
        ),
        name="local_grad",
    )(decay_rates, residues, grad_out)
    cross = pl.pallas_call(
        functools.partial(half_kernel, batch_count, half, mask),
        in_specs=[whole, whole],
        out_specs=whole,
        out_shape=jax.ShapeDtypeStruct(((batch_count + 1) * pieces, modes, width), jnp.float32),
        compiler_params=params(),
        name="half",
    )(local_grad, terms)
    other = lax.ppermute(cross, "seq", [(s, (s + half) % block_count) for s in range(block_count)])
    back = pl.pallas_call(
        functools.partial(scan_kernel, batch_count, half, mask, paired),
        in_specs=[whole] * 4,
        out_specs=whole,
        out_shape=jax.ShapeDtypeStruct((owners, pieces * modes + total_rows, width), jnp.float32),
        compiler_params=params(),
        name="scan",
    )(local_grad, terms, cross, other)
    back = from_owners(reorder(exchange(back)), chunks)
    return pl.pallas_call(
        functools.partial(finish_kernel, 4, read_incoming, read_total),
        in_specs=[whole] * 3,
        out_specs=[anywhere, anywhere],
        out_shape=[
            jax.ShapeDtypeStruct((1, rows, channels), jnp.bfloat16),
            jax.ShapeDtypeStruct((modes, channels // batch_count), jnp.float32),
        ],
        scratch_shapes=[
            pltpu.VMEM((rows, channels), jnp.bfloat16),
            pltpu.VMEM((modes, channels // batch_count), jnp.float32),
            pltpu.SemaphoreType.DMA((5,)),
        ],
        compiler_params=params(),
        name="finish",
    )(residues, local_grad, back)


def solution(mesh):
    placed = (P("dp", "seq", None), P("dp", "seq", None), P(), P())
    return jax.shard_map(
        functools.partial(local, mesh.shape["dp"], mesh.shape["seq"]),
        mesh=mesh,
        in_specs=placed,
        out_specs=(P("dp", "seq", None), P(None, "dp")),
        check_vma=False,
    )
```
